128 devices in a mesh: ctx: 32 (over y, z, x_lo), head: 4 (over x_hi, core).
Axes of the slice: x: 4 (x_hi: 2, x_lo: 2; x = x_hi * 2 + x_lo), y: 4, z: 4, core: 2. Of those that a mesh axis runs over, the one named last changes fastest.
Arguments:
- x_in: bfloat16 [49152, 8192], P('ctx', 'head'), may hold values from -6 to 6
- b_in: bfloat16 [49152, 1024], P('ctx', 'head'), may hold values from -6 to 6
- c_in: bfloat16 [49152, 1024], P('ctx', 'head'), may hold values from -6 to 6
- conv_x: bfloat16 [4, 8192], P(None, 'head'), may hold values from -3 to 3
- conv_b: bfloat16 [4, 1024], P(None, 'head'), may hold values from -3 to 3
- conv_c: bfloat16 [4, 1024], P(None, 'head'), may hold values from -3 to 3
- step_size: float32 [49152, 128], P('ctx', 'head'), may hold values from 0.0022552745 to 13.30215
- decay_rate: float32 [128], P('head'), may hold values from 0.0011276372 to 8.313844
- skip: float32 [128], P('head'), may hold values from 0.5 to 2
- gate: bfloat16 [49152, 8192], P('ctx', 'head'), may hold values from -200 to 200
- norm_gain: bfloat16 [8192], P('head'), may hold values from 0.099609375 to 1.8984375
- doc_starts: int32 [4], replicated, may hold values from 0 to 49151, as said below
Outputs:
- mixed: bfloat16 [49152, 8192], P('ctx', 'head')
The draws below stay inside these ranges and needn't reach their ends.
Inputs may be any that keep to these rules, and one draw needn't show every extreme that they name: `doc_starts`: strictly increasing; the first entry is 0 and the last is 49151, so the last document is the single final token.
All inputs are finite; a program needn't handle non-finite values.
Results may differ from the reference program's by a relative error of at most 0.0042.
Values may be sent and summed in bfloat16 or wider, within the bound.
A program may use at most 192 MiB of HBM per device.

```python
import math
import jax
import jax.numpy as jnp
from jax import lax

H = 128
P_SIZE = 64
N = 128
G = 8
K = 4
Q = 768
DOCS = 4
TOKENS = 49152


def draw_step_size(key, part):
    key = jax.random.fold_in(key, 11)
    base = TOKENS ** (-0.5)
    rough = jax.random.uniform(key, (TOKENS, H), jnp.float32, 0.5, 1.5)
    spots = jax.random.randint(jax.random.fold_in(key, 1), (3,), 0, TOKENS)
    offset = jnp.arange(TOKENS, dtype=jnp.int32)[:, None] - spots[None, :]
    hit = jnp.any((offset >= 0) & (offset < 8), axis=1)
    return jnp.where(hit[:, None], 0.04 * TOKENS ** 0.5 * rough, base * rough)


def draw_decay_rate(key, part):
    key = jax.random.fold_in(key, 12)
    base = TOKENS ** (-0.5)
    pick = jax.random.uniform(key, (H,), jnp.float32)
    level = jax.random.uniform(jax.random.fold_in(key, 1), (H,), jnp.float32, 0.5, 1.5)
    share = 0.35
    fast = level / (40.0 * base)
    slow = 0.5 * level / (TOKENS * base)
    return jnp.where(pick < share, fast, slow)


def draw_gate(key, part):
    key = jax.random.fold_in(key, 13)
    columns = jnp.arange(H * P_SIZE, dtype=jnp.float32) / (H * P_SIZE)
    row_scale = 10.0 ** jax.random.uniform(jax.random.fold_in(key, 1), (TOKENS, 1), jnp.float32)
    values = jnp.clip(jax.random.normal(key, (TOKENS, H * P_SIZE), jnp.float32), -4.0, 4.0)
    return (values * 0.5 * (10.0 ** columns)[None, :] * row_scale).astype(jnp.bfloat16)


def draw_doc_starts(key, part):
    key = jax.random.fold_in(key, 14)
    picks = jax.random.choice(key, TOKENS - 2, (DOCS - 2,), replace=False) + 1
    first = jnp.zeros((1,), jnp.int32)
    final = jnp.full((1,), TOKENS - 1, jnp.int32)
    return jnp.concatenate([first, jnp.sort(picks).astype(jnp.int32), final])


def shard_levels(rng, shape, split, low, high):
    level = 1.0
    for axis_at, blocks in split:
        draws = jax.random.uniform(jax.random.fold_in(jax.random.fold_in(rng, 6), axis_at), (blocks,), jnp.float32, low / len(split), high / len(split))
        level = level * jnp.repeat(jnp.exp(draws), shape[axis_at] // blocks).reshape((-1,) + (1,) * (len(shape) - 1 - axis_at))
    return level


def bell_draw(key, shape, deviation, bound, split=(), kind=jnp.bfloat16):
    values = jax.random.normal(key, shape, jnp.float32) * deviation
    if len(split) > 0:
        values = shard_levels(key, shape, split, -0.22, 0.18) * values
    return jnp.clip(values, min=-bound, max=bound).astype(kind)


def setup_inputs(seed: int = 0) -> dict:
    key_of = jax.random.split(jax.random.key(seed), 13)
    x_in = bell_draw(key_of[0], (TOKENS, H * P_SIZE), 1.0, 6.0, ((0, 32), (1, 4)))
    b_in = bell_draw(key_of[1], (TOKENS, G * N), 1.0, 6.0, ((0, 32), (1, 4)))
    c_in = bell_draw(key_of[2], (TOKENS, G * N), 1.0, 6.0, ((0, 32), (1, 4)))
    conv_x = bell_draw(key_of[3], (K, H * P_SIZE), K ** -0.5, 3.0, ((1, 4),))
    conv_b = bell_draw(key_of[4], (K, G * N), K ** -0.5, 3.0, ((1, 4),))
    conv_c = bell_draw(key_of[5], (K, G * N), K ** -0.5, 3.0, ((1, 4),))
    step_size = draw_step_size(jax.random.fold_in(key_of[12], 71), 0)
    decay_rate = draw_decay_rate(jax.random.fold_in(key_of[12], 71), 0)
    skip = jnp.clip(jnp.exp(math.log(2.0) - 1.3862944 * jax.random.uniform(key_of[8], (H,), jnp.float32) ** shard_levels(key_of[8], (H,), ((0, 4),), -0.2, 0.2)), 0.5, 2.0)
    gate = draw_gate(jax.random.fold_in(key_of[12], 71), 0)
    norm_gain = jnp.clip(1.0 + 0.18 * jax.random.normal(key_of[10], (H * P_SIZE,), jnp.float32), 0.099609375, 1.8984375).astype(jnp.bfloat16)
    doc_starts = draw_doc_starts(jax.random.fold_in(key_of[12], 71), 0)
    return {"x_in": x_in, "b_in": b_in, "c_in": c_in, "conv_x": conv_x, "conv_b": conv_b, "conv_c": conv_c, "step_size": step_size, "decay_rate": decay_rate, "skip": skip, "gate": gate, "norm_gain": norm_gain, "doc_starts": doc_starts}


EPS = 1e-05

def segment_ids(doc_starts, positions):
    return lax.optimization_barrier(jnp.sum((positions[:, None] >= doc_starts[None, :]).astype(jnp.int32), axis=1)) - 1

def conv_silu(padded, taps, seg_padded, row_count):
    seg_now = seg_padded[K - 1:]
    summed = jnp.zeros((row_count, padded.shape[1]), jnp.float32)
    for tap_index in range(K):
        window = padded[tap_index:tap_index + row_count].astype(jnp.float32)
        keeper = (seg_padded[tap_index:tap_index + row_count] == seg_now)[:, None]
        summed = summed + jnp.where(keeper, window * taps[tap_index].astype(jnp.float32)[None, :], 0.0)
    return jax.nn.silu(summed).astype(jnp.bfloat16)

def block_terms(x_conv, b_conv, c_conv, step, rate, skip, segment, seg_before):
    row_count = x_conv.shape[0]
    head_count = step.shape[1]
    groups = b_conv.shape[1] // N
    per_group = head_count // groups
    x_heads = x_conv.reshape(row_count, groups, per_group, P_SIZE).astype(jnp.float32)
    b_groups = b_conv.reshape(row_count, groups, N).astype(jnp.float32)
    c_groups = c_conv.reshape(row_count, groups, N).astype(jnp.float32)
    log_decay = jnp.cumsum(-step * rate[None, :], axis=0)
    position = jnp.arange(row_count, dtype=jnp.int32)
    allowed = (position[:, None] >= position[None, :]) & (segment[:, None] == segment[None, :])
    pieces = []
    for group_index in range(groups):
        head_start = group_index * per_group
        cum_t = log_decay[:, head_start:head_start + per_group].T
        decays = jnp.where(allowed[None], jnp.exp(jnp.minimum(cum_t[:, :, None] - cum_t[:, None, :], 0.0)), 0.0)
        scores = jnp.einsum('in,jn->ij', c_groups[:, group_index], b_groups[:, group_index])
        weights = (scores[None] * decays * step[:, head_start:head_start + per_group].T[:, None, :]).astype(jnp.bfloat16)
        pieces.append(jnp.einsum('kij,jkp->ikp', weights.astype(jnp.float32), x_heads[:, group_index]))
    intra = jnp.stack(pieces, axis=1)
    last_row = row_count - 1
    end_weight = jnp.where((segment == segment[last_row])[:, None], jnp.exp(log_decay[last_row][None, :] - log_decay), 0.0) * step
    weighted_b = (b_groups[:, :, None, :] * end_weight.reshape(row_count, groups, per_group)[:, :, :, None]).astype(jnp.bfloat16)
    local_state = jnp.einsum('jgkn,jgkp->gknp', weighted_b.astype(jnp.float32), x_heads)
    carry = jnp.where(segment[last_row] == seg_before, jnp.exp(log_decay[last_row]), 0.0)
    inflow = jnp.where((segment == seg_before)[:, None], jnp.exp(log_decay), 0.0)
    part = intra + skip.reshape(1, groups, per_group, 1) * x_heads
    return (part.reshape(row_count, -1), local_state, carry, inflow)

def cross_term(c_conv, state_in, inflow):
    row_count = c_conv.shape[0]
    groups = state_in.shape[0]
    c_groups = c_conv.reshape(row_count, groups, N).astype(jnp.float32)
    result = jnp.einsum('ign,gknp->igkp', c_groups, state_in, precision=lax.Precision.HIGHEST)
    return (result * inflow.reshape(row_count, groups, -1)[:, :, :, None]).reshape(row_count, -1)

def reference(x_in, b_in, c_in, conv_x, conv_b, conv_c, step_size, decay_rate, skip, gate, norm_gain, doc_starts):
    total_rows = x_in.shape[0]
    block_count = total_rows // Q
    rim_rows = K - 1
    positions = jnp.arange(total_rows + rim_rows, dtype=jnp.int32) - rim_rows
    seg_pad = segment_ids(doc_starts, positions)
    x_pad = jnp.pad(x_in, ((rim_rows, 0), (0, 0)))
    b_pad = jnp.pad(b_in, ((rim_rows, 0), (0, 0)))
    c_pad = jnp.pad(c_in, ((rim_rows, 0), (0, 0)))
    head_count = step_size.shape[1]
    groups = b_in.shape[1] // N
    gain_f = norm_gain.astype(jnp.float32)

    def one_block(state_in, index):
        start = index * Q
        seg_window = lax.dynamic_slice_in_dim(seg_pad, start, Q + rim_rows)
        x_conv = conv_silu(lax.dynamic_slice_in_dim(x_pad, start, Q + rim_rows, 0), conv_x, seg_window, Q)
        b_conv = conv_silu(lax.dynamic_slice_in_dim(b_pad, start, Q + rim_rows, 0), conv_b, seg_window, Q)
        c_conv = conv_silu(lax.dynamic_slice_in_dim(c_pad, start, Q + rim_rows, 0), conv_c, seg_window, Q)
        step = lax.dynamic_slice_in_dim(step_size, start, Q, 0)
        gate_now = lax.dynamic_slice_in_dim(gate, start, Q, 0)
        part, local_state, carry, inflow = block_terms(x_conv, b_conv, c_conv, step, decay_rate, skip, seg_window[rim_rows:], seg_window[rim_rows - 1])
        result = part + cross_term(c_conv, state_in, inflow)
        gated = result * jax.nn.silu(gate_now.astype(jnp.float32))
        meansq = lax.optimization_barrier(jnp.mean(gated * gated, axis=1, keepdims=True))
        mixed = (gated * lax.rsqrt(meansq + EPS) * gain_f[None, :]).astype(jnp.bfloat16)
        next_state = carry.reshape(groups, -1)[:, :, None, None] * state_in + local_state
        return (next_state, mixed)
    initial = jnp.zeros((groups, head_count // groups, N, P_SIZE), jnp.float32)
    final_state, blocks_out = lax.scan(one_block, initial, jnp.arange(block_count, dtype=jnp.int32))
    return blocks_out.reshape(total_rows, -1)
```

```python
import functools
import math

import jax
import jax.numpy as jnp
from jax import lax
from jax.experimental import pallas as pl
from jax.experimental.pallas import tpu as pltpu
from jax.sharding import PartitionSpec as P

F32 = jnp.float32
BF16 = jnp.bfloat16
P_SIZE = 64
N = 128
K = 4
L = 128
TILE = 256
EPS = 1e-05
LOG2E = math.log2(math.e)
HI = lax.Precision.HIGHEST
MESH = pl.DeviceIdType.MESH
PIECES = 32
ROWS = 80
FIRST_PART = 13


def silu(v):
    return v * (0.5 + 0.5 * jnp.tanh(0.5 * v))


def split3(v):
    hi = v.astype(BF16)
    rest = v - hi.astype(F32)
    mid = rest.astype(BF16)
    low = (rest - mid.astype(F32)).astype(BF16)
    return hi, mid, low


def wide3(v):
    return jnp.concatenate([p.astype(F32) for p in split3(v)], axis=1).astype(BF16)


def dot(a, b, **kw):
    return jnp.dot(a, b, preferred_element_type=F32, **kw)


def kernel(
    n_ctx,
    n_head,
    chunks,
    x_hbm,
    b_hbm,
    c_hbm,
    gate_hbm,
    taps_x,
    taps_b,
    taps_c,
    step_ref,
    rate_ref,
    skip_ref,
    doc_ref,
    gated_hbm,
    scale_ref,
    xbuf,
    bcbuf,
    gate_buf,
    xconv,
    bconv,
    cconv,
    yint,
    prefix,
    state,
    pcar,
    cum_s,
    cumt_s,
    allow_s,
    emask_s,
    sel,
    band,
    tril,
    send1,
    recv1,
    send2,
    recv2,
    sums,
    sums_recv,
    x_sem,
    bc_sem,
    gate_sem,
    out_sem,
    halo_ssem,
    halo_rsem,
    ssem1,
    rsem1,
    ssem2,
    rsem2,
    sum_ssem,
    sum_rsem,
):
    me = lax.axis_index("ctx")
    my_head = lax.axis_index("head")
    rows = chunks * L
    heads = step_ref.shape[1]
    per_dev = PIECES // n_ctx

    def x_copy(c):
        r = pl.ds(pl.multiple_of(c * L, L), L)
        d = pl.ds(pl.multiple_of(c * L + L, L), L)
        return pltpu.make_async_copy(x_hbm.at[r, :], xbuf.at[d, :], x_sem.at[c])

    def gate_copy(c):
        r = pl.ds(pl.multiple_of(c * L, L), L)
        return pltpu.make_async_copy(gate_hbm.at[r, :], gate_buf.at[r, :], gate_sem.at[c])

    b_copy = pltpu.make_async_copy(b_hbm, bcbuf.at[0, pl.ds(L, rows), :], bc_sem.at[0])
    c_copy = pltpu.make_async_copy(c_hbm, bcbuf.at[1, pl.ds(L, rows), :], bc_sem.at[1])
    b_copy.start()
    c_copy.start()

    def start_x(c, _):
        x_copy(c).start()
        return 0

    lax.fori_loop(0, chunks, start_x, 0)

    barrier = pltpu.get_barrier_semaphore()

    def greet_ctx(s, _):
        pl.semaphore_signal(
            barrier, inc=1, device_id={"ctx": lax.rem(me + s, n_ctx)}, device_id_type=MESH
        )
        return 0

    def greet_head(s, _):
        pl.semaphore_signal(
            barrier, inc=1, device_id={"head": lax.rem(my_head + s, n_head)}, device_id_type=MESH
        )
        return 0

    lax.fori_loop(1, n_ctx, greet_ctx, 0)
    lax.fori_loop(1, n_head, greet_head, 0)

    sel_row = lax.broadcasted_iota(jnp.int32, sel.shape, 0)
    sel_lane = lax.broadcasted_iota(jnp.int32, sel.shape, 1)
    sel[...] = jnp.where(
        lax.rem(sel_row, heads) == lax.div(sel_lane, P_SIZE), 1.0, 0.0
    ).astype(BF16)
    t_iota = lax.broadcasted_iota(jnp.int32, (L, L), 0)
    q_iota = lax.broadcasted_iota(jnp.int32, (L, L), 1)
    for s in range(1, K):
        band[s - 1, 0] = jnp.where(q_iota == t_iota + L - s, 1.0, 0.0)
        band[s - 1, 1] = jnp.where(q_iota == t_iota - s, 1.0, 0.0)
    tril[...] = jnp.where(t_iota >= q_iota, 1.0, 0.0)
    xbuf[0 : L - 16, :] = jnp.zeros((L - 16, xbuf.shape[1]), BF16)
    bcbuf[:, 0 : L - 16, :] = jnp.zeros((2, L - 16, bcbuf.shape[2]), BF16)
    state[...] = jnp.zeros_like(state)
    sums[...] = jnp.zeros_like(sums)

    pl.semaphore_wait(barrier, n_ctx + n_head - 2)

    rim = pl.ds(rows - 16, 16)
    spot = pl.ds(L - 16, 16)

    def halo(i):
        src = (x_hbm, b_hbm, c_hbm)[i].at[rim, :]
        dst = xbuf.at[spot, :] if i == 0 else bcbuf.at[i - 1, spot, :]
        return pltpu.make_async_remote_copy(
            src_ref=src,
            dst_ref=dst,
            send_sem=halo_ssem.at[i],
            recv_sem=halo_rsem.at[i],
            device_id={"ctx": lax.rem(me + 1, n_ctx)},
            device_id_type=MESH,
        )

    for i in range(3):
        halo(i).start()

    def start_gate(c, _):
        gate_copy(c).start()
        return 0

    lax.fori_loop(0, chunks, start_gate, 0)

    docs = [doc_ref[d] for d in range(doc_ref.shape[0])]

    def seg(pos):
        total = jnp.where(pos >= docs[0], 1, 0)
        for d in docs[1:]:
            total = total + jnp.where(pos >= d, 1, 0)
        return total

    b_copy.wait()
    c_copy.wait()
    for i in range(3):
        halo(i).wait_recv()

    def first(c, _):
        x_copy(c).wait()
        base = me * rows + c * L
        seg_t = seg(base + t_iota)
        seg_cur = seg(base + q_iota)
        seg_old = seg(base - L + q_iota)
        same_cur = seg_t == seg_cur
        same_old = seg_t == seg_old
        shifts = jnp.concatenate(
            [
                jnp.concatenate(
                    [
                        jnp.where(same_old, band[s, 0], 0.0),
                        jnp.where(same_cur, band[s, 1], 0.0),
                    ],
                    axis=1,
                ).astype(BF16)
                for s in range(K - 1)
            ],
            axis=0,
        )
        allow_s[c] = jnp.where(same_cur, tril[...], 0.0)
        window = pl.ds(pl.multiple_of(c * L, L), 2 * L)

        def conv(win, taps):
            moved = dot(shifts, win)
            v = moved[2 * L : 3 * L] * taps[0:1]
            v = v + moved[L : 2 * L] * taps[1:2]
            v = v + moved[0:L] * taps[2:3]
            v = v + win[L : 2 * L].astype(F32) * taps[3:4]
            return silu(v)

        b_now = conv(bcbuf[0, window, :], taps_b[...].astype(F32))
        c_now = conv(bcbuf[1, window, :], taps_c[...].astype(F32))
        groups = b_now.shape[1] // N
        b_t = []
        for g in range(groups):
            lanes = slice(g * N, (g + 1) * N)
            bconv[c * groups + g] = b_now[:, lanes].astype(BF16)
            cconv[c * groups + g] = c_now[:, lanes].astype(BF16)
            b_t.append(b_now[:, lanes].T.astype(BF16))

        step = step_ref[pl.ds(pl.multiple_of(c * L, L), L), :]
        cum = dot(tril[...], step * (rate_ref[...] * -LOG2E), precision=HI)
        cum_j = cum - jnp.log(step) * LOG2E
        cum_jt = cum_j.T
        per_group = heads // groups
        for g in range(groups):
            hs = slice(g * per_group, (g + 1) * per_group)
            cum_s[c * groups + g] = cum[:, hs]
            cumt_s[c * groups + g] = cum_jt[hs, :]
        seg_last = seg(base + L - 1)
        seg_before = seg(base - 1)
        cum_last = cum[L - 1 : L, :]
        h_iota = lax.broadcasted_iota(jnp.int32, (L, heads), 0)
        seg_h = seg(base + h_iota)
        weight = jnp.where(seg_h == seg_last, jnp.exp2(cum_last - cum_j), 0.0)
        emask_s[c] = jnp.where(seg_h == seg_before, jnp.exp2(cum), 0.0)
        carry = jnp.where(seg_last == seg_before, jnp.exp2(cum_last), 0.0)
        left = wide3(
            jnp.concatenate([weight, jnp.broadcast_to(carry, (16, heads))], axis=0)
        )
        for tile in range(x_hbm.shape[1] // TILE):
            lanes = slice(tile * TILE, (tile + 1) * TILE)
            g, at = divmod(tile * TILE, per_group * P_SIZE)
            here = slice(at, at + TILE)
            x_now = conv(xbuf[window, lanes], taps_x[:, lanes].astype(F32)).astype(BF16)
            xconv[c * groups + g, :, here] = x_now
            spread = dot(left, sel[:, lanes])
            x_weighted = (x_now.astype(F32) * spread[0:L]).astype(BF16)
            local = dot(b_t[g], x_weighted)
            factor = spread[L : L + 8]
            before = state[g, :, here]
            prefix[c * groups + g, :, here] = before
            state[g, :, here] = before * factor[0:1] + local
            old = jnp.where(c == 0, 1.0, pcar[c, :, lanes])
            pcar[c, :, lanes] = old
            pcar[c + 1, :, lanes] = old * factor
        return 0

    lax.fori_loop(0, chunks, first, 0)
    groups = bconv.shape[0] // chunks
    per_group = heads // groups

    r_iota = lax.broadcasted_iota(jnp.int32, (16, 128), 0)
    for pair in range(PIECES // 2):
        g, at = divmod(pair * 128, per_group * P_SIZE)
        hi, mid, low = split3(
            jnp.broadcast_to(pcar[chunks, 0:1, pair * 128 : (pair + 1) * 128], (16, 128))
        )
        tail = jnp.where(
            r_iota == 0,
            hi.astype(F32),
            jnp.where(r_iota == 1, mid.astype(F32), jnp.where(r_iota == 2, low.astype(F32), 0.0)),
        ).astype(BF16)
        for half in range(2):
            k = pair * 2 + half
            send1[k // per_dev, k % per_dev, 0:64, :] = state[
                g, half * 64 : (half + 1) * 64, at : at + 128
            ].astype(BF16)
            send1[k // per_dev, k % per_dev, 64:80, :] = tail

    def copy1(other, slot):
        return pltpu.make_async_remote_copy(
            src_ref=send1.at[other],
            dst_ref=recv1.at[slot],
            send_sem=ssem1.at[other],
            recv_sem=rsem1.at[slot],
            device_id={"ctx": other},
            device_id_type=MESH,
        )

    def copy2(other, slot):
        return pltpu.make_async_remote_copy(
            src_ref=send2.at[other],
            dst_ref=recv2.at[slot],
            send_sem=ssem2.at[other],
            recv_sem=rsem2.at[slot],
            device_id={"ctx": other},
            device_id_type=MESH,
        )

    def send_state(s, _):
        copy1(lax.rem(me + s, n_ctx), me).start()
        return 0

    lax.fori_loop(1, n_ctx, send_state, 0)
    recv1[me] = send1[me]

    lane = lax.broadcasted_iota(jnp.int32, (L, 128), 1)

    def second(i, _):
        c = lax.div(i, groups)
        scores = lax.dot_general(
            cconv[i], bconv[i], (((1,), (1,)), ((), ())), preferred_element_type=F32
        )
        scores = scores * allow_s[c]
        cum = cum_s[i]
        for pair in range(per_group // 2):
            ws = []
            for h in (2 * pair, 2 * pair + 1):
                gap = cum[:, h : h + 1] - cumt_s[i, h : h + 1, :]
                ws.append((scores * jnp.exp2(jnp.minimum(gap, 4.0))).astype(BF16))
            x_pair = xconv[i, :, pair * 128 : (pair + 1) * 128]
            zero = jnp.zeros_like(x_pair)
            both = jnp.concatenate(
                [jnp.where(lane < P_SIZE, x_pair, zero), jnp.where(lane < P_SIZE, zero, x_pair)],
                axis=0,
            )
            yint[i, :, pair * 128 : (pair + 1) * 128] = dot(jnp.concatenate(ws, axis=1), both)
        return 0

    lax.fori_loop(0, FIRST_PART, second, 0)

    def scan(e, acc):
        @pl.when(e != me)
        def _():
            copy1(e, e).wait_recv()

        out = []
        for k in range(per_dev):
            send2[e, k] = acc[k].astype(BF16)
            got = recv1[e, k].astype(F32)
            factor = got[64:65] + got[65:66] + got[66:67]
            out.append(acc[k] * factor + got[0:64])

        @pl.when(e != me)
        def _():
            copy2(e, me).start()

        @pl.when(e == me)
        def _():
            recv2[me] = send2[me]

        return tuple(out)

    lax.fori_loop(
        0, n_ctx, scan, tuple(jnp.zeros((64, 128), F32) for _ in range(per_dev))
    )
    lax.fori_loop(FIRST_PART, chunks * groups, second, 0)

    def take(s, _):
        copy2(me, lax.rem(me + s, n_ctx)).wait_recv()
        return 0

    lax.fori_loop(1, n_ctx, take, 0)

    ones = jnp.ones((8, 128), F32)

    def third(c, _):
        gate_copy(c).wait()
        r = pl.ds(pl.multiple_of(c * L, L), L)
        left = wide3(emask_s[c])
        skip3 = wide3(jnp.broadcast_to(skip_ref[...], (16, heads)))
        left = jnp.concatenate([left, skip3], axis=0)
        squares = jnp.zeros((L, 128), F32)
        for tile in range(x_hbm.shape[1] // TILE):
            lanes = slice(tile * TILE, (tile + 1) * TILE)
            g, at = divmod(tile * TILE, per_group * P_SIZE)
            here = slice(at, at + TILE)
            i = c * groups + g
            pieces = []
            for pair in (2 * tile, 2 * tile + 1):
                pieces.append(
                    jnp.concatenate(
                        [
                            recv2[k // per_dev, k % per_dev].astype(F32)
                            for k in (2 * pair, 2 * pair + 1)
                        ],
                        axis=0,
                    )
                )
            incoming = jnp.concatenate(pieces, axis=1)
            full = prefix[i, :, here] + pcar[c, 0:1, lanes] * incoming
            inter = dot(cconv[i], full.astype(BF16))
            spread = dot(left, sel[:, lanes])
            y = (
                yint[i, :, here]
                + spread[0:L] * inter
                + spread[L : L + 1] * xconv[i, :, here].astype(F32)
            )
            gated = y * silu(gate_buf[r, lanes].astype(F32))
            gate_buf[r, lanes] = gated.astype(BF16)
            sq = gated * gated
            squares = squares + sq[:, 0:128] + sq[:, 128:256]
        total = lax.dot_general(
            ones, squares, (((1,), (1,)), ((), ())), precision=HI, preferred_element_type=F32
        )
        sums[c] = total
        pltpu.make_async_copy(gate_buf.at[r, :], gated_hbm.at[r, :], out_sem.at[c]).start()
        return 0

    lax.fori_loop(0, chunks, third, 0)

    def sum_copy(other, slot):
        return pltpu.make_async_remote_copy(
            src_ref=sums,
            dst_ref=sums_recv.at[slot],
            send_sem=sum_ssem.at[other],
            recv_sem=sum_rsem.at[slot],
            device_id={"head": other},
            device_id_type=MESH,
        )

    def send_sum(s, _):
        sum_copy(lax.rem(my_head + s, n_head), my_head).start()
        return 0

    lax.fori_loop(1, n_head, send_sum, 0)

    def wait_out(c, _):
        r = pl.ds(pl.multiple_of(c * L, L), L)
        pltpu.make_async_copy(gate_buf.at[r, :], gated_hbm.at[r, :], out_sem.at[c]).wait()
        return 0

    def wait_sends(s, _):
        other = lax.rem(me + s, n_ctx)
        copy1(other, me).wait_send()
        copy2(other, me).wait_send()
        return 0

    lax.fori_loop(1, n_ctx, wait_sends, 0)
    for i in range(3):
        halo(i).wait_send()
    sums_recv[my_head] = sums[...]

    def take_sum(s, _):
        sum_copy(my_head, lax.rem(my_head + s, n_head)).wait_recv()
        return 0

    lax.fori_loop(1, n_head, take_sum, 0)
    total = sums_recv[0, :, 0, :]
    for k in range(1, n_head):
        total = total + sums_recv[k, :, 0, :]
    columns = n_head * heads * P_SIZE
    scale_ref[...] = lax.rsqrt(total / columns + EPS)

    def wait_sum(s, _):
        sum_copy(lax.rem(my_head + s, n_head), my_head).wait_send()
        return 0

    lax.fori_loop(1, n_head, wait_sum, 0)
    lax.fori_loop(0, chunks, wait_out, 0)


def solution(mesh):
    n_ctx = mesh.shape["ctx"]
    n_head = mesh.shape["head"]

    def shards(
        x_in, b_in, c_in, conv_x, conv_b, conv_c, step_size, decay_rate, skip, gate, norm_gain, doc_starts
    ):
        rows, cols = x_in.shape
        heads = step_size.shape[1]
        groups = b_in.shape[1] // N
        chunks = rows // L
        per_dev = PIECES // n_ctx
        wide = cols // groups
        per_group = heads // groups
        any_spec = pl.BlockSpec(memory_space=pl.ANY)
        vmem = pl.BlockSpec(memory_space=pltpu.VMEM)
        gated, scale = pl.pallas_call(
            functools.partial(kernel, n_ctx, n_head, chunks),
            out_shape=(
                jax.ShapeDtypeStruct((rows, cols), BF16),
                jax.ShapeDtypeStruct((chunks, L), F32),
            ),
            in_specs=[any_spec] * 4
            + [vmem] * 6
            + [pl.BlockSpec(memory_space=pltpu.SMEM)],
            out_specs=(any_spec, vmem),
            scratch_shapes=[
                pltpu.VMEM((rows + L, cols), BF16),
                pltpu.VMEM((2, rows + L, groups * N), BF16),
                pltpu.VMEM((rows, cols), BF16),
                pltpu.VMEM((chunks * groups, L, wide), BF16),
                pltpu.VMEM((chunks * groups, L, N), BF16),
                pltpu.VMEM((chunks * groups, L, N), BF16),
                pltpu.VMEM((chunks * groups, L, wide), F32),
                pltpu.VMEM((chunks * groups, N, wide), F32),
                pltpu.VMEM((groups, N, wide), F32),
                pltpu.VMEM((chunks + 1, 8, cols), F32),
                pltpu.VMEM((chunks * groups, L, per_group), F32),
                pltpu.VMEM((chunks * groups, per_group, L), F32),
                pltpu.VMEM((chunks, L, L), F32),
                pltpu.VMEM((chunks, L, heads), F32),
                pltpu.VMEM((3 * heads, cols), BF16),
                pltpu.VMEM((K - 1, 2, L, L), F32),
                pltpu.VMEM((L, L), F32),
                pltpu.VMEM((n_ctx, per_dev, ROWS, 128), BF16),
                pltpu.VMEM((n_ctx, per_dev, ROWS, 128), BF16),
                pltpu.VMEM((n_ctx, per_dev, 64, 128), BF16),
                pltpu.VMEM((n_ctx, per_dev, 64, 128), BF16),
                pltpu.VMEM((chunks, 8, L), F32),
                pltpu.VMEM((n_head, chunks, 8, L), F32),
                pltpu.SemaphoreType.DMA((chunks,)),
                pltpu.SemaphoreType.DMA((2,)),
                pltpu.SemaphoreType.DMA((chunks,)),
                pltpu.SemaphoreType.DMA((chunks,)),
                pltpu.SemaphoreType.DMA((3,)),
                pltpu.SemaphoreType.DMA((3,)),
                pltpu.SemaphoreType.DMA((n_ctx,)),
                pltpu.SemaphoreType.DMA((n_ctx,)),
                pltpu.SemaphoreType.DMA((n_ctx,)),
                pltpu.SemaphoreType.DMA((n_ctx,)),
                pltpu.SemaphoreType.DMA((n_head,)),
                pltpu.SemaphoreType.DMA((n_head,)),
            ],
            compiler_params=pltpu.CompilerParams(
                collective_id=0, has_side_effects=True, vmem_limit_bytes=62 * 1024 * 1024
            ),
        )(
            x_in,
            b_in,
            c_in,
            gate,
            conv_x,
            conv_b,
            conv_c,
            step_size,
            decay_rate.reshape(1, -1),
            skip.reshape(1, -1),
            doc_starts,
        )
        return (
            gated.astype(F32) * scale.reshape(rows, 1) * norm_gain.astype(F32)[None, :]
        ).astype(BF16)

    split = P("ctx", "head")
    taps = P(None, "head")
    line = P("head")
    return jax.shard_map(
        shards,
        mesh=mesh,
        in_specs=(split,) * 3 + (taps,) * 3 + (split, line, line, split, line, P()),
        out_specs=split,
        check_vma=False,
    )
```

```python
import functools
import math

import jax
import jax.numpy as jnp
from jax import lax
from jax.experimental import pallas as pl
from jax.experimental.pallas import tpu as pltpu
from jax.sharding import PartitionSpec as P

F32 = jnp.float32
BF16 = jnp.bfloat16
P_SIZE = 64
N = 128
K = 4
L = 128
TILE = 256
CONV_TILE = 128
EPS = 1e-05
LOG2E = math.log2(math.e)
HI = lax.Precision.HIGHEST
MESH = pl.DeviceIdType.MESH
PIECES = 32
ROWS = 80
FIRST_PART = 12


def split3(v):
    hi = v.astype(BF16)
    rest = v - hi.astype(F32)
    mid = rest.astype(BF16)
    low = (rest - mid.astype(F32)).astype(BF16)
    return hi, mid, low


def dot(a, b, **kw):
    return jnp.dot(a, b, preferred_element_type=F32, **kw)


def kernel(
    n_ctx,
    n_head,
    chunks,
    x_hbm,
    b_hbm,
    c_hbm,
    gate_hbm,
    taps_x,
    taps_b,
    taps_c,
    step_ref,
    rate_ref,
    skip_ref,
    gain_ref,
    doc_ref,
    gate_buf,
    xbuf,
    bcbuf,
    yint,
    xconv,
    cconv,
    prefix,
    state,
    pcar,
    cum_all,
    cum_s,
    cumt_s,
    allow_s,
    scores_s,
    keep_s,
    left_s,
    carries,
    factors,
    sel,
    send1,
    recv1,
    send2,
    recv2,
    squares_s,
    sums,
    sums_recv,
    x_sem,
    bc_sem,
    gate_sem,
    halo_ssem,
    halo_rsem,
    ssem1,
    rsem1,
    ssem2,
    rsem2,
    sum_ssem,
    sum_rsem,
):
    me = lax.axis_index("ctx")
    my_head = lax.axis_index("head")
    rows = chunks * L
    heads = step_ref.shape[0]
    per_dev = PIECES // n_ctx

    def x_copy(c):
        r = pl.ds(pl.multiple_of(c * L, L), L)
        d = pl.ds(pl.multiple_of(c * L + L, L), L)
        return pltpu.make_async_copy(x_hbm.at[r, :], xbuf.at[d, :], x_sem.at[c])

    gate_copy = pltpu.make_async_copy(gate_hbm, gate_buf, gate_sem)
    b_copy = pltpu.make_async_copy(b_hbm, bcbuf.at[0, pl.ds(L, rows), :], bc_sem.at[0])
    c_copy = pltpu.make_async_copy(c_hbm, bcbuf.at[1, pl.ds(L, rows), :], bc_sem.at[1])
    b_copy.start()
    c_copy.start()

    def start_x(c, _):
        x_copy(c).start()
        return 0

    lax.fori_loop(0, 2, start_x, 0)

    barrier = pltpu.get_barrier_semaphore()

    def greet_ctx(s, _):
        pl.semaphore_signal(
            barrier, inc=1, device_id={"ctx": lax.rem(me + s, n_ctx)}, device_id_type=MESH
        )
        return 0

    def greet_head(s, _):
        pl.semaphore_signal(
            barrier, inc=1, device_id={"head": lax.rem(my_head + s, n_head)}, device_id_type=MESH
        )
        return 0

    lax.fori_loop(1, n_ctx, greet_ctx, 0)
    lax.fori_loop(1, n_head, greet_head, 0)

    sel_row = lax.broadcasted_iota(jnp.int32, (L, x_hbm.shape[1]), 0)
    sel_lane = lax.broadcasted_iota(jnp.int32, (L, x_hbm.shape[1]), 1)
    chosen = jnp.where(lax.rem(sel_row, heads) == lax.div(sel_lane, P_SIZE), 1.0, 0.0)
    sel[0] = jnp.where(sel_row < 2 * heads, chosen, 0.0).astype(BF16)
    sel[1] = jnp.where(sel_row >= 2 * heads, chosen, 0.0).astype(BF16)
    sel[2] = jnp.where(sel_row < 3 * heads, chosen, 0.0).astype(BF16)
    t_iota = lax.broadcasted_iota(jnp.int32, (L, L), 0)
    q_iota = lax.broadcasted_iota(jnp.int32, (L, L), 1)
    xbuf[0 : L - 16, :] = jnp.zeros((L - 16, xbuf.shape[1]), BF16)
    bcbuf[:, 0 : L - 16, :] = jnp.zeros((2, L - 16, bcbuf.shape[2]), BF16)
    state[...] = jnp.zeros_like(state)
    sums[...] = jnp.zeros_like(sums)
    groups = cconv.shape[0] // chunks
    per_group = heads // groups
    docs = [doc_ref[d] for d in range(doc_ref.shape[0])]

    def seg(pos):
        total = jnp.where(pos >= docs[0], 1, 0)
        for d in docs[1:]:
            total = total + jnp.where(pos >= d, 1, 0)
        return total

    pl.semaphore_wait(barrier, n_ctx + n_head - 2)

    rim = pl.ds(rows - 16, 16)
    spot = pl.ds(L - 16, 16)

    def halo(i):
        src = (x_hbm, b_hbm, c_hbm)[i].at[rim, :]
        dst = xbuf.at[spot, :] if i == 0 else bcbuf.at[i - 1, spot, :]
        return pltpu.make_async_remote_copy(
            src_ref=src,
            dst_ref=dst,
            send_sem=halo_ssem.at[i],
            recv_sem=halo_rsem.at[i],
            device_id={"ctx": lax.rem(me + 1, n_ctx)},
            device_id_type=MESH,
        )

    for i in range(3):
        halo(i).start()

    lax.fori_loop(2, chunks, start_x, 0)

    gate_copy.start()

    eye = lax.broadcasted_iota(jnp.int32, (heads, heads), 0) == lax.broadcasted_iota(
        jnp.int32, (heads, heads), 1
    )

    def column(row):
        return jnp.sum(
            jnp.where(eye, jnp.broadcast_to(row, (heads, heads)), 0.0), axis=1, keepdims=True
        )

    rate = column(rate_ref[...]) * -LOG2E
    steps = [step_ref[:, c * L : (c + 1) * L] for c in range(chunks)]
    triu = jnp.where(t_iota <= q_iota, 1.0, 0.0)
    cum_all[...] = dot(jnp.concatenate([v * rate for v in steps], axis=0), triu, precision=HI)
    carries[...] = jnp.where(
        lax.broadcasted_iota(jnp.int32, (heads, L), 1) == chunks, column(skip_ref[...]), 0.0
    )

    def decays(c, _):
        base = me * rows + c * L
        here = pl.ds(pl.multiple_of(c * heads, heads), heads)
        cum = cum_all[here, :]
        step = step_ref[:, pl.ds(pl.multiple_of(c * L, L), L)]
        cum_j = cum - jnp.log(step) * LOG2E
        h_lane = lax.broadcasted_iota(jnp.int32, (heads, L), 1)
        seg_j = seg(base + h_lane)
        seg_last = seg(base + L - 1)
        seg_before = seg(base - 1)
        last = cum[:, L - 1 : L]
        weight = jnp.where(seg_j == seg_last, jnp.exp2(last - cum_j), 0.0)
        inflow = jnp.where(seg_j == seg_before, jnp.exp2(cum), 0.0)
        carry = jnp.where(seg_last == seg_before, jnp.exp2(last), 0.0)
        carries[...] = jnp.where(h_lane == c, carry, carries[...])
        w_hi = weight.astype(BF16).astype(F32)
        i_hi = inflow.astype(BF16).astype(F32)
        stack = jnp.concatenate([w_hi, weight - w_hi, i_hi, inflow - i_hi], axis=0)
        left_s[c] = stack.T.astype(BF16)
        cum_t = jnp.concatenate([cum, jnp.zeros((L - heads, L), F32)], axis=0).T
        for g in range(groups):
            hs = slice(g * per_group, (g + 1) * per_group)
            cum_s[c * groups + g] = cum_t[:, hs]
            cumt_s[c * groups + g] = cum_j[hs, :]
        seg_t = seg(base + t_iota)
        seg_q = seg(base + lax.broadcasted_iota(jnp.int32, (1, L), 1))
        allow_s[c] = jnp.where(jnp.logical_and(seg_t == seg_q, t_iota >= q_iota), 1.0, 0.0)
        since = jnp.full((L, L), 4, jnp.int32)
        for d in docs:
            gap = base + t_iota - d
            since = jnp.minimum(since, jnp.where(gap < 0, 4, gap))
        for s in range(1, K):
            keep_s[c, s - 1] = jnp.where(since < s, 0.0, 1.0)
        return 0

    lax.fori_loop(0, chunks, decays, 0)
    c_hi, c_mid, c_low = split3(carries[...])
    c_all = jnp.concatenate(
        [v.astype(F32) for v in (c_hi, c_mid, c_low)] + [jnp.zeros((L - 3 * heads, L), F32)], axis=0
    )
    factors[...] = dot(c_all.T.astype(BF16)[0:16, :], sel[2])

    b_copy.wait()
    c_copy.wait()
    for i in range(3):
        halo(i).wait_recv()

    def conv(win, taps, keep):
        w = win.astype(F32)
        half = taps * 0.5
        v = (pltpu.roll(w, 3, 0)[16:] * keep[2]) * half[0:1]
        v = v + (pltpu.roll(w, 2, 0)[16:] * keep[1]) * half[1:2]
        v = v + (pltpu.roll(w, 1, 0)[16:] * keep[0]) * half[2:3]
        v = v + w[16:] * half[3:4]
        return v + v * jnp.tanh(v)

    def first(c, _, w=True):
        if w:
            x_copy(c).wait()
        window = pl.ds(pl.multiple_of(c * L + L - 16, 16), L + 16)
        keep = [keep_s[c, s] for s in range(K - 1)]
        left = left_s[c]
        b_t = []
        for g in range(groups):
            lanes = slice(g * N, (g + 1) * N)
            b_now = conv(bcbuf[0, window, lanes], taps_b[:, lanes].astype(F32), keep)
            b_t.append(b_now.T.astype(BF16))
            c_now = conv(bcbuf[1, window, lanes], taps_c[:, lanes].astype(F32), keep).astype(BF16)
            cconv[c * groups + g] = c_now
            scores_s[c * groups + g] = allow_s[c] * dot(c_now, b_t[g])
        for tile in range(x_hbm.shape[1] // TILE):
            lanes = slice(tile * TILE, (tile + 1) * TILE)
            g, at = divmod(tile * TILE, per_group * P_SIZE)
            here = slice(at, at + TILE)
            spread = dot(left, sel[0, :, lanes])
            parts = []
            for half in range(TILE // 128):
                sub = slice(tile * TILE + half * 128, tile * TILE + (half + 1) * 128)
                x_now = conv(xbuf[window, sub], taps_x[:, sub].astype(F32), keep).astype(BF16)
                xconv[c * groups + g, :, at + half * 128 : at + (half + 1) * 128] = x_now
                parts.append(
                    (x_now.astype(F32) * spread[:, half * 128 : (half + 1) * 128]).astype(BF16)
                )
            local = dot(b_t[g], jnp.concatenate(parts, axis=1))
            factor = factors[pl.ds(c, 1), lanes]
            before = state[g, :, here]
            prefix[c * groups + g, :, here] = before
            state[g, :, here] = before * factor + local
            old = jnp.where(c == 0, 1.0, pcar[c, 0:1, lanes])
            pcar[c, 0:1, lanes] = old
            pcar[c + 1, 0:1, lanes] = old * factor
        return 0

    lax.fori_loop(0, chunks, first, 0)

    r_iota = lax.broadcasted_iota(jnp.int32, (16, 128), 0)
    for pair in range(PIECES // 2):
        g, at = divmod(pair * 128, per_group * P_SIZE)
        hi, mid, low = split3(
            jnp.broadcast_to(pcar[chunks, 0:1, pair * 128 : (pair + 1) * 128], (16, 128))
        )
        tail = jnp.where(
            r_iota == 0,
            hi.astype(F32),
            jnp.where(r_iota == 1, mid.astype(F32), jnp.where(r_iota == 2, low.astype(F32), 0.0)),
        ).astype(BF16)
        for half in range(2):
            k = pair * 2 + half
            send1[k // per_dev, k % per_dev, 0:64, :] = state[
                g, half * 64 : (half + 1) * 64, at : at + 128
            ].astype(BF16)
            send1[k // per_dev, k % per_dev, 64:80, :] = tail

    def copy1(other):
        return pltpu.make_async_remote_copy(
            src_ref=send1.at[other],
            dst_ref=recv1.at[me],
            send_sem=ssem1,
            recv_sem=rsem1,
            device_id={"ctx": other},
            device_id_type=MESH,
        )

    def copy2(other):
        return pltpu.make_async_remote_copy(
            src_ref=send2.at[other],
            dst_ref=recv2.at[me],
            send_sem=ssem2,
            recv_sem=rsem2,
            device_id={"ctx": other},
            device_id_type=MESH,
        )

    def all_of(send, recv, ssem, rsem):
        some = pl.ds(0, n_ctx - 1)
        return pltpu.make_async_remote_copy(
            src_ref=send.at[some],
            dst_ref=recv.at[some],
            send_sem=ssem,
            recv_sem=rsem,
            device_id={"ctx": lax.rem(me + 1, n_ctx)},
            device_id_type=MESH,
        )

    all1 = all_of(send1, recv1, ssem1, rsem1)
    all2 = all_of(send2, recv2, ssem2, rsem2)

    def send_state(s, _):
        copy1(lax.rem(me + s, n_ctx)).start()
        return 0

    lax.fori_loop(1, n_ctx, send_state, 0)
    recv1[me] = send1[me]

    lane = lax.broadcasted_iota(jnp.int32, (L, 128), 1)

    def second(i, _):
        c = lax.div(i, groups)
        scores = scores_s[i]
        cum = cum_s[i]
        for pair in range(per_group // 2):
            ws = []
            for h in (2 * pair, 2 * pair + 1):
                gap = cum[:, h : h + 1] - cumt_s[i, h : h + 1, :]
                ws.append((scores * jnp.exp2(jnp.minimum(gap, 4.0))).astype(BF16))
            x_pair = xconv[i, :, pair * 128 : (pair + 1) * 128]
            zero = jnp.zeros_like(x_pair)
            both = jnp.concatenate(
                [jnp.where(lane < P_SIZE, x_pair, zero), jnp.where(lane < P_SIZE, zero, x_pair)],
                axis=0,
            )
            yint[i, :, pair * 128 : (pair + 1) * 128] = dot(jnp.concatenate(ws, axis=1), both)
        return 0

    lax.fori_loop(0, FIRST_PART, second, 0, unroll=4)

    all1.wait_recv()

    def scan(e, acc):
        out = []
        for k in range(per_dev):
            send2[e, k] = acc[k].astype(BF16)
            got = recv1[e, k].astype(F32)
            factor = got[64:65] + got[65:66] + got[66:67]
            out.append(acc[k] * factor + got[0:64])
        return tuple(out)

    lax.fori_loop(
        0, n_ctx, scan, tuple(jnp.zeros((64, 128), F32) for _ in range(per_dev)), unroll=4
    )

    def send_back(s, _):
        copy2(lax.rem(me + s, n_ctx)).start()
        return 0

    lax.fori_loop(1, n_ctx, send_back, 0)
    recv2[me] = send2[me]
    lax.fori_loop(FIRST_PART, chunks * groups, second, 0, unroll=4)

    all2.wait_recv()

    def sum_copy(part, other):
        some = pl.ds(part * 8, 8)
        return pltpu.make_async_remote_copy(
            src_ref=sums.at[some, :],
            dst_ref=sums_recv.at[my_head, some, :],
            send_sem=sum_ssem.at[part],
            recv_sem=sum_rsem.at[part],
            device_id={"head": other},
            device_id_type=MESH,
        )

    def sums_in(part):
        some = pl.ds(part * 8, 8)
        whole = sums_recv.at[pl.ds(0, n_head - 1), some, :]
        return pltpu.make_async_remote_copy(
            src_ref=whole,
            dst_ref=whole,
            send_sem=sum_ssem.at[part],
            recv_sem=sum_rsem.at[part],
            device_id={"head": lax.rem(my_head + 1, n_head)},
            device_id_type=MESH,
        )

    def send_sums(part):
        for s in range(1, n_head):
            sum_copy(part, lax.rem(my_head + s, n_head)).start()
        some = slice(part * 8, part * 8 + 8)
        sums_recv[my_head, some, :] = sums[some, :]

    def add_up(c):
        total = jnp.sum(squares_s[lax.rem(c, 2)].T, axis=0, keepdims=True)
        sums[pl.ds(c, 1), :] = total

    def third(c, _, w=True, skip_sum=False):
        if not skip_sum:
            add_up(c - 1)
        r = pl.ds(pl.multiple_of(c * L, L), L)
        squares = jnp.zeros((L, 128), F32)
        for tile in range(x_hbm.shape[1] // TILE):
            lanes = slice(tile * TILE, (tile + 1) * TILE)
            g, at = divmod(tile * TILE, per_group * P_SIZE)
            here = slice(at, at + TILE)
            i = c * groups + g
            pieces = []
            for pair in (2 * tile, 2 * tile + 1):
                pieces.append(
                    jnp.concatenate(
                        [
                            recv2[k // per_dev, k % per_dev].astype(F32)
                            for k in (2 * pair, 2 * pair + 1)
                        ],
                        axis=0,
                    )
                )
            incoming = jnp.concatenate(pieces, axis=1)
            full = prefix[i, :, here] + pcar[c, 0:1, lanes] * incoming
            inter = dot(cconv[i], full.astype(BF16))
            spread = dot(left_s[c], sel[1, :, lanes])
            y = (
                yint[i, :, here]
                + spread * inter
                + factors[chunks : chunks + 1, lanes] * xconv[i, :, here].astype(F32)
            )
            v = gate_buf[r, lanes].astype(F32) * 0.5
            gated = y * (v + v * jnp.tanh(v))
            yint[i, :, here] = gated
            sq = gated * gated
            squares = squares + sq[:, 0:128] + sq[:, 128:256]
        squares_s[lax.rem(c, 2)] = squares
        return 0

    gate_copy.wait()
    third(0, 0, skip_sum=True)
    lax.fori_loop(1, 9, third, 0)
    send_sums(0)
    lax.fori_loop(9, chunks, third, 0)
    add_up(chunks - 1)
    send_sums(1)

    all1.wait_send()
    all2.wait_send()
    for i in range(3):
        halo(i).wait_send()

    columns = n_head * heads * P_SIZE

    def norm(c, _):
        total = sums_recv[0, pl.ds(c, 1), :]
        for k in range(1, n_head):
            total = total + sums_recv[k, pl.ds(c, 1), :]
        row = lax.rsqrt(total / columns + EPS)
        scale = jnp.broadcast_to(row, (L, L)).T
        r = pl.ds(pl.multiple_of(c * L, L), L)
        for at in range(0, x_hbm.shape[1], L):
            g, off = divmod(at, per_group * P_SIZE)
            gain = gain_ref[at : at + L].astype(F32)[None, :]
            value = yint[c * groups + g, :, off : off + L] * scale * gain
            gate_buf[r, at : at + L] = value.astype(BF16)
        return 0

    sums_in(0).wait_recv()
    lax.fori_loop(0, 8, norm, 0)
    sums_in(1).wait_recv()
    lax.fori_loop(8, chunks, norm, 0)
    sums_in(0).wait_send()
    sums_in(1).wait_send()


def store(chunks, from_ref, out_hbm, sem):
    def copy(c):
        r = pl.ds(pl.multiple_of(c * L, L), L)
        return pltpu.make_async_copy(from_ref.at[r, :], out_hbm.at[r, :], sem.at[c])

    def begin(c, _):
        copy(c).start()
        return 0

    def finish(c, _):
        copy(c).wait()
        return 0

    lax.fori_loop(0, chunks, begin, 0)
    lax.fori_loop(0, chunks, finish, 0)


def solution(mesh):
    n_ctx = mesh.shape["ctx"]
    n_head = mesh.shape["head"]

    def shards(
        x_in, b_in, c_in, conv_x, conv_b, conv_c, step_size, decay_rate, skip, gate, norm_gain, doc_starts
    ):
        rows, cols = x_in.shape
        heads = step_size.shape[1]
        groups = b_in.shape[1] // N
        chunks = rows // L
        per_dev = PIECES // n_ctx
        wide = cols // groups
        per_group = heads // groups
        any_spec = pl.BlockSpec(memory_space=pl.ANY)
        vmem = pl.BlockSpec(memory_space=pltpu.VMEM)
        mixed = pl.pallas_call(
            functools.partial(kernel, n_ctx, n_head, chunks),
            out_shape=pltpu.VMEM((rows, cols), BF16),
            in_specs=[any_spec] * 4
            + [vmem] * 7
            + [pl.BlockSpec(memory_space=pltpu.SMEM)],
            out_specs=vmem,
            scratch_shapes=[
                pltpu.VMEM((rows + L, cols), BF16),
                pltpu.VMEM((2, rows + L, groups * N), BF16),
                pltpu.VMEM((chunks * groups, L, wide), F32),
                pltpu.VMEM((chunks * groups, L, wide), BF16),
                pltpu.VMEM((chunks * groups, L, N), BF16),
                pltpu.VMEM((chunks * groups, N, wide), F32),
                pltpu.VMEM((groups, N, wide), F32),
                pltpu.VMEM((chunks + 1, 8, cols), F32),
                pltpu.VMEM((chunks * heads, L), F32),
                pltpu.VMEM((chunks * groups, L, per_group), F32),
                pltpu.VMEM((chunks * groups, per_group, L), F32),
                pltpu.VMEM((chunks, L, L), F32),
                pltpu.VMEM((chunks * groups, L, L), F32),
                pltpu.VMEM((chunks, K - 1, L, L), F32),
                pltpu.VMEM((chunks, L, L), BF16),
                pltpu.VMEM((heads, L), F32),
                pltpu.VMEM((16, cols), F32),
                pltpu.VMEM((3, L, cols), BF16),
                pltpu.VMEM((n_ctx, per_dev, ROWS, 128), BF16),
                pltpu.VMEM((n_ctx, per_dev, ROWS, 128), BF16),
                pltpu.VMEM((n_ctx, per_dev, 64, 128), BF16),
                pltpu.VMEM((n_ctx, per_dev, 64, 128), BF16),
                pltpu.VMEM((2, L, 128), F32),
                pltpu.VMEM((16, L), F32),
                pltpu.VMEM((n_head, 16, L), F32),
                pltpu.SemaphoreType.DMA((chunks,)),
                pltpu.SemaphoreType.DMA((2,)),
                pltpu.SemaphoreType.DMA,
                pltpu.SemaphoreType.DMA((3,)),
                pltpu.SemaphoreType.DMA((3,)),
                pltpu.SemaphoreType.DMA,
                pltpu.SemaphoreType.DMA,
                pltpu.SemaphoreType.DMA,
                pltpu.SemaphoreType.DMA,
                pltpu.SemaphoreType.DMA((2,)),
                pltpu.SemaphoreType.DMA((2,)),
            ],
            compiler_params=pltpu.CompilerParams(
                collective_id=0, has_side_effects=True, vmem_limit_bytes=56 * 1024 * 1024
            ),
        )(
            x_in,
            b_in,
            c_in,
            gate,
            conv_x,
            conv_b,
            conv_c,
            step_size.T,
            decay_rate.reshape(1, -1),
            skip.reshape(1, -1),
            norm_gain,
            doc_starts,
        )
        return pl.pallas_call(
            functools.partial(store, chunks),
            out_shape=jax.ShapeDtypeStruct((rows, cols), BF16),
            in_specs=[vmem],
            out_specs=any_spec,
            scratch_shapes=[pltpu.SemaphoreType.DMA((chunks,))],
            compiler_params=pltpu.CompilerParams(vmem_limit_bytes=24 * 1024 * 1024),
        )(mixed)

    split = P("ctx", "head")
    taps = P(None, "head")
    line = P("head")
    return jax.shard_map(
        shards,
        mesh=mesh,
        in_specs=(split,) * 3 + (taps,) * 3 + (split, line, line, split, line, P()),
        out_specs=split,
        check_vma=False,
    )
```

```python
import functools
import math

import jax
import jax.numpy as jnp
from jax import lax
from jax.experimental import pallas as pl
from jax.experimental.pallas import tpu as pltpu
from jax.sharding import PartitionSpec as P

F32 = jnp.float32
BF16 = jnp.bfloat16
P_SIZE = 64
N = 128
K = 4
RIM = 16
L = 128
TILE = 256
CONV_TILE = 128
EPS = 1e-05
LOG2E = math.log2(math.e)
HI = lax.Precision.HIGHEST
MESH = pl.DeviceIdType.MESH
PIECES = 16
ROWS = 80
FIRST_PART = 24


def split3(v):
    hi = v.astype(BF16)
    rest = v - hi.astype(F32)
    mid = rest.astype(BF16)
    low = (rest - mid.astype(F32)).astype(BF16)
    return hi, mid, low


def dot(a, b, **kw):
    return jnp.dot(a, b, preferred_element_type=F32, **kw)


def kernel(
    n_ctx,
    n_head,
    chunks,
    x_hbm,
    b_hbm,
    c_hbm,
    gate_hbm,
    taps_x,
    taps_b,
    taps_c,
    step_ref,
    rate_ref,
    skip_ref,
    gain_ref,
    doc_ref,
    gate_buf,
    conv_s,
    xbuf,
    bcbuf,
    yint,
    xconv,
    cconv,
    prefix,
    state,
    start_s,
    pcar,
    cum_all,
    cum_s,
    cumt_s,
    allow_s,
    scores_s,
    keep_s,
    left_s,
    carries,
    factors,
    sel,
    send1,
    recv1,
    send2,
    recv2,
    squares_s,
    sums,
    sums_recv,
    x_sem,
    bc_sem,
    gate_sem,
    halo_ssem,
    halo_rsem,
    ssem1,
    rsem1,
    ssem2,
    rsem2,
    sum_ssem,
    sum_rsem,
):
    me = lax.axis_index("ctx")
    my_head = lax.axis_index("head")
    rows = chunks * L
    heads = step_ref.shape[0]
    owners = max(n_ctx // 2, 1)
    per_dev = PIECES // owners
    split = n_ctx == 32

    def x_copy(c):
        r = pl.ds(pl.multiple_of(c * L, L), L)
        d = pl.ds(pl.multiple_of(c * L + RIM, RIM), L)
        return pltpu.make_async_copy(x_hbm.at[r, :], xbuf.at[d, :], x_sem.at[c])

    gate_copy = pltpu.make_async_copy(gate_hbm, gate_buf, gate_sem)
    b_copy = pltpu.make_async_copy(b_hbm, bcbuf.at[0, pl.ds(RIM, rows), :], bc_sem.at[0])
    c_copy = pltpu.make_async_copy(c_hbm, bcbuf.at[1, pl.ds(RIM, rows), :], bc_sem.at[1])
    b_copy.start()
    c_copy.start()

    def start_x(c, _):
        x_copy(c).start()
        return 0

    lax.fori_loop(0, chunks, start_x, 0)
    gate_copy.start()

    barrier = pltpu.get_barrier_semaphore()

    def greet_ctx(s, _):
        pl.semaphore_signal(
            barrier, inc=1, device_id={"ctx": lax.rem(me + s, n_ctx)}, device_id_type=MESH
        )
        return 0

    def greet_head(s, _):
        pl.semaphore_signal(
            barrier, inc=1, device_id={"head": lax.rem(my_head + s, n_head)}, device_id_type=MESH
        )
        return 0

    lax.fori_loop(1, n_ctx, greet_ctx, 0)
    lax.fori_loop(1, n_head, greet_head, 0)

    sel_row = lax.broadcasted_iota(jnp.int32, (L, x_hbm.shape[1]), 0)
    sel_lane = lax.broadcasted_iota(jnp.int32, (L, x_hbm.shape[1]), 1)
    chosen = jnp.where(lax.rem(sel_row, heads) == lax.div(sel_lane, P_SIZE), 1.0, 0.0)
    sel[0] = jnp.where(sel_row < 2 * heads, chosen, 0.0).astype(BF16)
    sel[1] = jnp.where(sel_row >= 2 * heads, chosen, 0.0).astype(BF16)
    sel[2] = jnp.where(sel_row < 3 * heads, chosen, 0.0).astype(BF16)
    t_iota = lax.broadcasted_iota(jnp.int32, (L, L), 0)
    q_iota = lax.broadcasted_iota(jnp.int32, (L, L), 1)
    pcar[0, 0:1, :] = jnp.zeros((1, pcar.shape[2]), F32)
    pcar[1, 0:1, :] = jnp.ones((1, pcar.shape[2]), F32)
    state[...] = jnp.zeros_like(state)
    sums[...] = jnp.zeros_like(sums)
    groups = cconv.shape[0] // chunks
    per_group = heads // groups
    docs = [doc_ref[d] for d in range(doc_ref.shape[0])]

    def seg(pos):
        total = jnp.where(pos >= docs[0], 1, 0)
        for d in docs[1:]:
            total = total + jnp.where(pos >= d, 1, 0)
        return total

    eye = lax.broadcasted_iota(jnp.int32, (heads, heads), 0) == lax.broadcasted_iota(
        jnp.int32, (heads, heads), 1
    )

    def column(row):
        return jnp.sum(
            jnp.where(eye, jnp.broadcast_to(row, (heads, heads)), 0.0), axis=1, keepdims=True
        )

    rate = column(rate_ref[...]) * -LOG2E
    steps = [step_ref[:, c * L : (c + 1) * L] for c in range(chunks)]
    triu = jnp.where(t_iota <= q_iota, 1.0, 0.0)
    cum_all[...] = dot(jnp.concatenate([v * rate for v in steps], axis=0), triu, precision=HI)
    carries[...] = jnp.where(
        lax.broadcasted_iota(jnp.int32, (heads, L), 1) == chunks, column(skip_ref[...]), 0.0
    )

    def decays(c, _):
        base = me * rows + c * L
        here = pl.ds(pl.multiple_of(c * heads, heads), heads)
        cum = cum_all[here, :]
        step = step_ref[:, pl.ds(pl.multiple_of(c * L, L), L)]
        cum_j = cum - jnp.log(step) * LOG2E
        h_lane = lax.broadcasted_iota(jnp.int32, (heads, L), 1)
        seg_j = seg(base + h_lane)
        seg_last = seg(base + L - 1)
        seg_before = seg(base - 1)
        last = cum[:, L - 1 : L]
        weight = jnp.where(seg_j == seg_last, jnp.exp2(last - cum_j), 0.0)
        inflow = jnp.where(seg_j == seg_before, jnp.exp2(cum), 0.0)
        carry = jnp.where(seg_last == seg_before, jnp.exp2(last), 0.0)
        carries[...] = jnp.where(h_lane == c, carry, carries[...])
        w_hi = weight.astype(BF16).astype(F32)
        i_hi = inflow.astype(BF16).astype(F32)
        stack = jnp.concatenate([w_hi, weight - w_hi, i_hi, inflow - i_hi], axis=0)
        left_s[c] = stack.T.astype(BF16)
        cum_t = jnp.concatenate([cum, jnp.zeros((L - heads, L), F32)], axis=0).T
        for g in range(groups):
            hs = slice(g * per_group, (g + 1) * per_group)
            cum_s[c * groups + g] = cum_t[:, hs]
            cumt_s[c * groups + g] = cum_j[hs, :]
        seg_t = seg(base + t_iota)
        seg_q = seg(base + lax.broadcasted_iota(jnp.int32, (1, L), 1))
        allow_s[c] = jnp.where(jnp.logical_and(seg_t == seg_q, t_iota >= q_iota), 1.0, 0.0)
        since = jnp.full((L, L), 4, jnp.int32)
        for d in docs:
            gap = base + t_iota - d
            since = jnp.minimum(since, jnp.where(gap < 0, 4, gap))
        for s in range(1, K):
            keep_s[c, s - 1] = jnp.where(since < s, 0.0, 1.0)
        return 0

    lax.fori_loop(0, chunks, decays, 0, unroll=4)
    c_hi, c_mid, c_low = split3(carries[...])
    c_all = jnp.concatenate(
        [v.astype(F32) for v in (c_hi, c_mid, c_low)] + [jnp.zeros((L - 3 * heads, L), F32)], axis=0
    )
    factors[...] = dot(c_all.T.astype(BF16)[0:16, :], sel[2])

    rim = pl.ds(rows - RIM, RIM)
    spot = pl.ds(0, RIM)

    def halo(i):
        src = (x_hbm, b_hbm, c_hbm)[i].at[rim, :]
        dst = xbuf.at[spot, :] if i == 0 else bcbuf.at[i - 1, spot, :]
        return pltpu.make_async_remote_copy(
            src_ref=src,
            dst_ref=dst,
            send_sem=halo_ssem.at[i],
            recv_sem=halo_rsem.at[i],
            device_id={"ctx": lax.rem(me + 1, n_ctx)},
            device_id_type=MESH,
        )

    b_copy.wait()
    c_copy.wait()
    x_copy(0).wait()

    def conv(win, taps, keep, slot):
        w = win.astype(F32)
        cs = conv_s.at[slot]
        cs[...] = w
        half = taps * 0.5
        v = (cs[13 : 13 + L, :] * keep[2]) * half[0:1]
        v = v + (cs[14 : 14 + L, :] * keep[1]) * half[1:2]
        v = v + (cs[15 : 15 + L, :] * keep[0]) * half[2:3]
        v = v + w[16:] * half[3:4]
        return v + v * jnp.tanh(v)

    def first(g, w, c, _):
        at_start = isinstance(c, int)
        if w and not at_start:
            x_copy(c).wait()
        i = c * groups + g
        window = pl.ds(pl.multiple_of(c * L, L), L + RIM)
        keep = [keep_s[c, s] for s in range(K - 1)]
        left = left_s[c]
        mine = slice(g * N, (g + 1) * N)
        b_now = conv(bcbuf[0, window, mine], taps_b[:, mine].astype(F32), keep, 0)
        b_t = b_now.T.astype(BF16)
        c_now = conv(bcbuf[1, window, mine], taps_c[:, mine].astype(F32), keep, 1).astype(BF16)
        cconv[i] = c_now
        scores_s[i] = allow_s[c] * dot(c_now, b_t)
        wide = per_group * P_SIZE
        for at in range(0, wide, TILE):
            lanes = slice(g * wide + at, g * wide + at + TILE)
            here = slice(at, at + TILE)
            spread = dot(left, sel[0, :, lanes])
            parts = []
            for half in range(0, TILE, 128):
                sub = slice(lanes.start + half, lanes.start + half + 128)
                x_now = conv(xbuf[window, sub], taps_x[:, sub].astype(F32), keep, 2 + (at + half) // 128).astype(BF16)
                xconv[i, :, at + half : at + half + 128] = x_now
                parts.append((x_now.astype(F32) * spread[:, half : half + 128]).astype(BF16))
            local = dot(b_t, jnp.concatenate(parts, axis=1))
            if at_start:
                start_s[g, :, here] = local
                continue
            factor = factors[pl.ds(c, 1), lanes]
            before = state[g, :, here]
            prefix[i, :, here] = before
            state[g, :, here] = before * factor + local
            pcar[c + 1, 0:1, lanes] = pcar[c, 0:1, lanes] * factor
        return 0

    def owner(g, q):
        if not split:
            return q * min(n_ctx, 2) + (g if n_ctx > 1 else 0)
        y, z_hi, x = lax.div(q, 4), lax.rem(lax.div(q, 2), 2), lax.rem(q, 2)
        return (y * 4 + z_hi * 2 + lax.rem(y + g, 2)) * 2 + x

    if split:
        my_y, my_z = lax.div(me, 8), lax.rem(lax.div(me, 2), 4)
        my_g = lax.rem(my_y + my_z, 2)
        my_q = (my_y * 2 + lax.div(my_z, 2)) * 2 + lax.rem(me, 2)
    else:
        my_g, my_q = lax.rem(me, 2), lax.div(me, 2)

    def owns(g):
        return my_g == g if n_ctx > 1 else True

    r_iota = lax.broadcasted_iota(jnp.int32, (16, 128), 0)

    def copy1(g, q):
        return pltpu.make_async_remote_copy(
            src_ref=send1.at[g, q],
            dst_ref=recv1.at[me],
            send_sem=ssem1.at[g],
            recv_sem=rsem1,
            device_id={"ctx": owner(g, q)},
            device_id_type=MESH,
        )

    def copy2(g, other):
        return pltpu.make_async_remote_copy(
            src_ref=send2.at[other],
            dst_ref=recv2.at[g, my_q],
            send_sem=ssem2,
            recv_sem=rsem2.at[g],
            device_id={"ctx": other},
            device_id_type=MESH,
        )

    def bulk(ref, ssem, rsem):
        return pltpu.make_async_remote_copy(
            src_ref=ref,
            dst_ref=ref,
            send_sem=ssem,
            recv_sem=rsem,
            device_id={"ctx": lax.rem(me + 1, n_ctx)},
            device_id_type=MESH,
        )

    def send_state(g):
        for pair in range(PIECES // 2):
            here = slice(pair * 128, pair * 128 + 128)
            at = g * per_group * P_SIZE + pair * 128
            hi, mid, low = split3(
                jnp.broadcast_to(
                    pcar[chunks, 0:1, at : at + 128] * factors[0:1, at : at + 128], (16, 128)
                )
            )
            tail = jnp.where(
                r_iota == 0,
                hi.astype(F32),
                jnp.where(
                    r_iota == 1, mid.astype(F32), jnp.where(r_iota == 2, low.astype(F32), 0.0)
                ),
            ).astype(BF16)
            for half in range(2):
                q, k = divmod(pair * 2 + half, per_dev)
                part = slice(half * 64, (half + 1) * 64)
                send1[g, q, k, 0:64, :] = (
                    state[g, part, here]
                    + start_s[g, part, here] * pcar[chunks, 0:1, at : at + 128]
                ).astype(BF16)
                send1[g, q, k, 64:80, :] = tail

        def send(s, _):
            copy1(g, lax.rem(my_q + s, owners)).start()
            return 0

        if n_ctx > 1:
            lax.fori_loop(jnp.where(owns(g), 1, 0), owners, send, 0)

        @pl.when(owns(g))
        def _():
            recv1[me] = send1[g, my_q]

    def scan_state(g):
        @pl.when(owns(g))
        def _():
            if n_ctx > 1:
                bulk(recv1.at[pl.ds(0, n_ctx - 1)], ssem1.at[g], rsem1).wait_recv()

            def scan(e, acc):
                out = []
                for k in range(per_dev):
                    send2[e, k] = acc[k].astype(BF16)
                    got = recv1[e, k].astype(F32)
                    factor = got[64:65] + got[65:66] + got[66:67]
                    out.append(acc[k] * factor + got[0:64])
                return tuple(out)

            lax.fori_loop(
                0,
                n_ctx,
                scan,
                tuple(jnp.zeros((64, 128), F32) for _ in range(per_dev)),
                unroll=min(4, n_ctx),
            )

            def send_back(s, _):
                copy2(g, lax.rem(me + s, n_ctx)).start()
                return 0

            lax.fori_loop(1, n_ctx, send_back, 0)
            recv2[g, my_q] = send2[me]

    def wait_state(g):
        if n_ctx > 1:
            if owners > 1:

                @pl.when(owns(g))
                def _():
                    bulk(recv2.at[g, pl.ds(0, owners - 1)], ssem2, rsem2.at[g]).wait_recv()

            @pl.when(jnp.logical_not(owns(g)))
            def _():
                bulk(recv2.at[g], ssem2, rsem2.at[g]).wait_recv()

    def wait_sends():
        if n_ctx > 1:
            for g in range(groups):
                if owners > 1:

                    @pl.when(owns(g))
                    def _(g=g):
                        bulk(send1.at[g, pl.ds(0, owners - 1)], ssem1.at[g], rsem1).wait_send()

                @pl.when(jnp.logical_not(owns(g)))
                def _(g=g):
                    bulk(send1.at[g], ssem1.at[g], rsem1).wait_send()

            bulk(send2.at[pl.ds(0, n_ctx - 1)], ssem2, rsem2.at[0]).wait_send()

    lax.fori_loop(1, 6, functools.partial(first, 0, True), 0)
    pl.semaphore_wait(barrier, n_ctx + n_head - 2)
    for i in range(3):
        halo(i).start()
    lax.fori_loop(6, chunks, functools.partial(first, 0, True), 0)
    for i in range(3):
        halo(i).wait_recv()
    first(0, True, 0, 0)
    send_state(0)
    lax.fori_loop(1, chunks, functools.partial(first, 1, False), 0)
    first(1, False, 0, 0)
    send_state(1)
    scan_state(0)

    lane = lax.broadcasted_iota(jnp.int32, (L, 128), 1)

    def second(i, _):
        c = lax.div(i, groups)
        scores = scores_s[i]
        cum = cum_s[i]
        for pair in range(per_group // 2):
            ws = []
            for h in (2 * pair, 2 * pair + 1):
                gap = cum[:, h : h + 1] - cumt_s[i, h : h + 1, :]
                ws.append((scores * jnp.exp2(jnp.minimum(gap, 4.0))).astype(BF16))
            x_pair = xconv[i, :, pair * 128 : (pair + 1) * 128]
            zero = jnp.zeros_like(x_pair)
            both = jnp.concatenate(
                [jnp.where(lane < P_SIZE, x_pair, zero), jnp.where(lane < P_SIZE, zero, x_pair)],
                axis=0,
            )
            yint[i, :, pair * 128 : (pair + 1) * 128] = dot(jnp.concatenate(ws, axis=1), both)
        return 0

    lax.fori_loop(0, FIRST_PART, second, 0, unroll=4)
    scan_state(1)
    lax.fori_loop(FIRST_PART, chunks * groups, second, 0, unroll=4)

    def sum_copy(part, other):
        some = pl.ds(part * 8, 8)
        return pltpu.make_async_remote_copy(
            src_ref=sums.at[some, :],
            dst_ref=sums_recv.at[my_head, some, :],
            send_sem=sum_ssem.at[part],
            recv_sem=sum_rsem.at[part],
            device_id={"head": other},
            device_id_type=MESH,
        )

    def sums_in(part):
        some = pl.ds(part * 8, 8)
        whole = sums_recv.at[pl.ds(0, n_head - 1), some, :]
        return pltpu.make_async_remote_copy(
            src_ref=whole,
            dst_ref=whole,
            send_sem=sum_ssem.at[part],
            recv_sem=sum_rsem.at[part],
            device_id={"head": lax.rem(my_head + 1, n_head)},
            device_id_type=MESH,
        )

    def send_sums(part):
        for s in range(1, n_head):
            sum_copy(part, lax.rem(my_head + s, n_head)).start()
        some = slice(part * 8, part * 8 + 8)
        sums_recv[my_head, some, :] = sums[some, :]

    def add_up(c):
        total = jnp.sum(squares_s[c].T, axis=0, keepdims=True)
        sums[pl.ds(c, 1), :] = total

    def enter(g):
        wide = per_group * P_SIZE
        for pair in range(wide // 128):
            here = slice(pair * 128, (pair + 1) * 128)
            factor = factors[0:1, g * wide + here.start : g * wide + here.stop]
            for half in range(2):
                part = slice(half * 64, (half + 1) * 64)
                k = 2 * pair + half
                incoming = recv2[g, k // per_dev, k % per_dev].astype(F32)
                prefix[g, part, here] = incoming
                start_s[g, part, here] = start_s[g, part, here] + factor * incoming

    def third(g, c, _):
        i = c * groups + g
        r = pl.ds(pl.multiple_of(c * L, L), L)
        left = left_s[c]
        wide = per_group * P_SIZE
        squares = jnp.zeros((L, 128), F32) if g == 0 else squares_s[c]
        for at in range(0, wide, TILE):
            lanes = slice(g * wide + at, g * wide + at + TILE)
            here = slice(at, at + TILE)
            full = prefix[i, :, here] + pcar[c, 0:1, lanes] * start_s[g, :, here]
            inter = dot(cconv[i], full.astype(BF16))
            spread = dot(left, sel[1, :, lanes])
            y = (
                yint[i, :, here]
                + spread * inter
                + factors[chunks : chunks + 1, lanes] * xconv[i, :, here].astype(F32)
            )
            v = gate_buf[r, lanes].astype(F32) * 0.5
            gated = y * (v + v * jnp.tanh(v))
            yint[i, :, here] = gated
            sq = gated * gated
            squares = squares + sq[:, 0:128] + sq[:, 128:256]
        squares_s[c] = squares
        return 0

    def third_last(c, _):
        add_up(c - 1)
        return third(1, c, 0)

    gate_copy.wait()
    wait_state(0)
    enter(0)
    lax.fori_loop(0, chunks, functools.partial(third, 0), 0)
    wait_state(1)
    enter(1)
    third(1, 0, 0)
    lax.fori_loop(1, 9, third_last, 0)
    send_sums(0)
    lax.fori_loop(9, chunks, third_last, 0)
    add_up(chunks - 1)
    send_sums(1)

    wait_sends()
    for i in range(3):
        halo(i).wait_send()

    columns = n_head * heads * P_SIZE

    def norm(c, _):
        total = sums_recv[0, pl.ds(c, 1), :]
        for k in range(1, n_head):
            total = total + sums_recv[k, pl.ds(c, 1), :]
        row = lax.rsqrt(total / columns + EPS)
        scale = jnp.broadcast_to(row, (L, L)).T
        r = pl.ds(pl.multiple_of(c * L, L), L)
        for at in range(0, x_hbm.shape[1], L):
            g, off = divmod(at, per_group * P_SIZE)
            gain = gain_ref[at : at + L].astype(F32)[None, :]
            value = yint[c * groups + g, :, off : off + L] * scale * gain
            gate_buf[r, at : at + L] = value.astype(BF16)
        return 0

    sums_in(0).wait_recv()
    lax.fori_loop(0, 8, norm, 0)
    sums_in(1).wait_recv()
    lax.fori_loop(8, chunks, norm, 0)
    sums_in(0).wait_send()
    sums_in(1).wait_send()


def store(chunks, from_ref, out_hbm, sem):
    def copy(c):
        r = pl.ds(pl.multiple_of(c * L, L), L)
        return pltpu.make_async_copy(from_ref.at[r, :], out_hbm.at[r, :], sem.at[c])

    def begin(c, _):
        copy(c).start()
        return 0

    def finish(c, _):
        copy(c).wait()
        return 0

    lax.fori_loop(0, chunks, begin, 0)
    lax.fori_loop(0, chunks, finish, 0)


def solution(mesh):
    n_ctx = mesh.shape["ctx"]
    n_head = mesh.shape["head"]

    def shards(
        x_in, b_in, c_in, conv_x, conv_b, conv_c, step_size, decay_rate, skip, gate, norm_gain, doc_starts
    ):
        rows, cols = x_in.shape
        heads = step_size.shape[1]
        groups = b_in.shape[1] // N
        chunks = rows // L
        owners = max(n_ctx // 2, 1)
        per_dev = PIECES // owners
        wide = cols // groups
        per_group = heads // groups
        any_spec = pl.BlockSpec(memory_space=pl.ANY)
        vmem = pl.BlockSpec(memory_space=pltpu.VMEM)
        mixed = pl.pallas_call(
            functools.partial(kernel, n_ctx, n_head, chunks),
            out_shape=pltpu.VMEM((rows, cols), BF16),
            in_specs=[any_spec] * 4
            + [vmem] * 7
            + [pl.BlockSpec(memory_space=pltpu.SMEM)],
            out_specs=vmem,
            scratch_shapes=[
                pltpu.VMEM((10, L + 16, 128), F32),
                pltpu.VMEM((rows + RIM, cols), BF16),
                pltpu.VMEM((2, rows + RIM, groups * N), BF16),
                pltpu.VMEM((chunks * groups, L, wide), F32),
                pltpu.VMEM((chunks * groups, L, wide), BF16),
                pltpu.VMEM((chunks * groups, L, N), BF16),
                pltpu.VMEM((chunks * groups, N, wide), F32),
                pltpu.VMEM((groups, N, wide), F32),
                pltpu.VMEM((groups, N, wide), F32),
                pltpu.VMEM((chunks + 1, 8, cols), F32),
                pltpu.VMEM((chunks * heads, L), F32),
                pltpu.VMEM((chunks * groups, L, per_group), F32),
                pltpu.VMEM((chunks * groups, per_group, L), F32),
                pltpu.VMEM((chunks, L, L), F32),
                pltpu.VMEM((chunks * groups, L, L), F32),
                pltpu.VMEM((chunks, K - 1, L, L), F32),
                pltpu.VMEM((chunks, L, L), BF16),
                pltpu.VMEM((heads, L), F32),
                pltpu.VMEM((16, cols), F32),
                pltpu.VMEM((3, L, cols), BF16),
                pltpu.VMEM((groups, owners, per_dev, ROWS, 128), BF16),
                pltpu.VMEM((n_ctx, per_dev, ROWS, 128), BF16),
                pltpu.VMEM((n_ctx, per_dev, 64, 128), BF16),
                pltpu.VMEM((groups, owners, per_dev, 64, 128), BF16),
                pltpu.VMEM((chunks, L, 128), F32),
                pltpu.VMEM((16, L), F32),
                pltpu.VMEM((n_head, 16, L), F32),
                pltpu.SemaphoreType.DMA((chunks,)),
                pltpu.SemaphoreType.DMA((2,)),
                pltpu.SemaphoreType.DMA,
                pltpu.SemaphoreType.DMA((3,)),
                pltpu.SemaphoreType.DMA((3,)),
                pltpu.SemaphoreType.DMA((groups,)),
                pltpu.SemaphoreType.DMA,
                pltpu.SemaphoreType.DMA,
                pltpu.SemaphoreType.DMA((groups,)),
                pltpu.SemaphoreType.DMA((2,)),
                pltpu.SemaphoreType.DMA((2,)),
            ],
            compiler_params=pltpu.CompilerParams(
                collective_id=0, has_side_effects=True, vmem_limit_bytes=56 * 1024 * 1024
            ),
        )(
            x_in,
            b_in,
            c_in,
            gate,
            conv_x,
            conv_b,
            conv_c,
            step_size.T,
            decay_rate.reshape(1, -1),
            skip.reshape(1, -1),
            norm_gain,
            doc_starts,
        )
        return pl.pallas_call(
            functools.partial(store, chunks),
            out_shape=jax.ShapeDtypeStruct((rows, cols), BF16),
            in_specs=[vmem],
            out_specs=any_spec,
            scratch_shapes=[pltpu.SemaphoreType.DMA((chunks,))],
            compiler_params=pltpu.CompilerParams(vmem_limit_bytes=24 * 1024 * 1024),
        )(mixed)

    split = P("ctx", "head")
    taps = P(None, "head")
    line = P("head")
    return jax.shard_map(
        shards,
        mesh=mesh,
        in_specs=(split,) * 3 + (taps,) * 3 + (split, line, line, split, line, P()),
        out_specs=split,
        check_vma=False,
    )
```

```python
import functools
import math

import jax
import jax.numpy as jnp
from jax import lax
from jax.experimental import pallas as pl
from jax.experimental.pallas import tpu as pltpu
from jax.sharding import PartitionSpec as P

F32 = jnp.float32
BF16 = jnp.bfloat16
P_SIZE = 64
N = 128
K = 4
RIM = 16
L = 128
TILE = 256
CONV_TILE = 128
EPS = 1e-05
LOG2E = math.log2(math.e)
HI = lax.Precision.HIGHEST
MESH = pl.DeviceIdType.MESH
PIECES = 16
ROWS = 80
FIRST_PART = 24


def split3(v):
    hi = v.astype(BF16)
    rest = v - hi.astype(F32)
    mid = rest.astype(BF16)
    low = (rest - mid.astype(F32)).astype(BF16)
    return hi, mid, low


def dot(a, b, **kw):
    return jnp.dot(a, b, preferred_element_type=F32, **kw)


def kernel(
    n_ctx,
    n_head,
    chunks,
    x_hbm,
    b_hbm,
    c_hbm,
    gate_hbm,
    taps_x,
    taps_b,
    taps_c,
    step_ref,
    rate_ref,
    skip_ref,
    gain_ref,
    doc_ref,
    gate_buf,
    conv_s,
    xbuf,
    bcbuf,
    yint,
    xconv,
    cconv,
    prefix,
    start_s,
    pcar,
    cum_all,
    cum_s,
    cumt_s,
    allow_s,
    scores_s,
    keep_s,
    left_s,
    carries,
    factors,
    skip_s,
    sel,
    send1,
    recv1,
    send2,
    recv2,
    squares_s,
    sums,
    sums_recv,
    x_sem,
    bc_sem,
    gate_sem,
    halo_ssem,
    halo_rsem,
    ssem1,
    rsem1,
    ssem2,
    rsem2,
    sum_ssem,
    sum_rsem,
):
    me = lax.axis_index("ctx")
    my_head = lax.axis_index("head")
    rows = chunks * L
    heads = step_ref.shape[0]
    owners = max(n_ctx // 2, 1)
    per_dev = PIECES // owners
    split = n_ctx == 32

    def x_copy(c):
        r = pl.ds(pl.multiple_of(c * L, L), L)
        d = pl.ds(pl.multiple_of(c * L + RIM, RIM), L)
        return pltpu.make_async_copy(x_hbm.at[r, :], xbuf.at[d, :], x_sem.at[c])

    gate_copy = pltpu.make_async_copy(gate_hbm, gate_buf, gate_sem)
    b_copy = pltpu.make_async_copy(b_hbm, bcbuf.at[0, pl.ds(RIM, rows), :], bc_sem.at[0])
    c_copy = pltpu.make_async_copy(c_hbm, bcbuf.at[1, pl.ds(RIM, rows), :], bc_sem.at[1])
    b_copy.start()
    c_copy.start()

    def start_x(c, _):
        x_copy(c).start()
        return 0

    lax.fori_loop(0, chunks, start_x, 0)
    gate_copy.start()

    barrier = pltpu.get_barrier_semaphore()

    def greet_ctx(s, _):
        pl.semaphore_signal(
            barrier, inc=1, device_id={"ctx": lax.rem(me + s, n_ctx)}, device_id_type=MESH
        )
        return 0

    def greet_head(s, _):
        pl.semaphore_signal(
            barrier, inc=1, device_id={"head": lax.rem(my_head + s, n_head)}, device_id_type=MESH
        )
        return 0

    lax.fori_loop(1, n_ctx, greet_ctx, 0)
    lax.fori_loop(1, n_head, greet_head, 0)

    sel_row = lax.broadcasted_iota(jnp.int32, (L, x_hbm.shape[1]), 0)
    sel_lane = lax.broadcasted_iota(jnp.int32, (L, x_hbm.shape[1]), 1)
    chosen = jnp.where((sel_row & (heads - 1)) == (sel_lane >> 6), 1.0, 0.0)
    sel[0] = jnp.where(sel_row < 2 * heads, chosen, 0.0).astype(BF16)
    sel[1] = jnp.where(sel_row >= 2 * heads, chosen, 0.0).astype(BF16)
    sel[2] = jnp.where(sel_row < 3 * heads, chosen, 0.0).astype(BF16)
    t_iota = lax.broadcasted_iota(jnp.int32, (L, L), 0)
    q_iota = lax.broadcasted_iota(jnp.int32, (L, L), 1)
    pcar[0, 0:1, :] = jnp.zeros((1, pcar.shape[2]), F32)
    pcar[1, 0:1, :] = jnp.ones((1, pcar.shape[2]), F32)
    sums[...] = jnp.zeros_like(sums)
    groups = cconv.shape[0] // chunks
    per_group = heads // groups
    prefix[groups : 2 * groups] = jnp.zeros((groups,) + prefix.shape[1:], F32)
    docs = [doc_ref[d] for d in range(doc_ref.shape[0])]

    def seg(pos):
        total = jnp.where(pos >= docs[0], 1, 0)
        for d in docs[1:]:
            total = total + jnp.where(pos >= d, 1, 0)
        return total

    eye = lax.broadcasted_iota(jnp.int32, (heads, heads), 0) == lax.broadcasted_iota(
        jnp.int32, (heads, heads), 1
    )

    def column(row):
        return jnp.sum(
            jnp.where(eye, jnp.broadcast_to(row, (heads, heads)), 0.0), axis=1, keepdims=True
        )

    rate = column(rate_ref[...]) * -LOG2E
    steps = [step_ref[:, c * L : (c + 1) * L] for c in range(chunks)]
    triu = jnp.where(t_iota <= q_iota, 1.0, 0.0)
    cum_all[...] = dot(jnp.concatenate([v * rate for v in steps], axis=0), triu, precision=HI)
    carries[...] = jnp.where(
        lax.broadcasted_iota(jnp.int32, (heads, L), 1) == chunks, column(skip_ref[...]), 0.0
    )

    def decays(c, _):
        base = me * rows + c * L
        here = pl.ds(pl.multiple_of(c * heads, heads), heads)
        cum = cum_all[here, :]
        step = step_ref[:, pl.ds(pl.multiple_of(c * L, L), L)]
        cum_j = cum - jnp.log(step) * LOG2E
        h_lane = lax.broadcasted_iota(jnp.int32, (heads, L), 1)
        seg_j = seg(base + h_lane)
        seg_last = seg(base + L - 1)
        seg_before = seg(base - 1)
        last = cum[:, L - 1 : L]
        weight = jnp.where(seg_j == seg_last, jnp.exp2(last - cum_j), 0.0)
        inflow = jnp.where(seg_j == seg_before, jnp.exp2(cum), 0.0)
        carry = jnp.where(seg_last == seg_before, jnp.exp2(last), 0.0)
        carries[...] = jnp.where(h_lane == c, carry, carries[...])
        w_hi = weight.astype(BF16).astype(F32)
        i_hi = inflow.astype(BF16).astype(F32)
        stack = jnp.concatenate([w_hi, weight - w_hi, i_hi, inflow - i_hi], axis=0)
        left_s[c] = stack.T.astype(BF16)
        cum_t = jnp.concatenate([cum, jnp.zeros((L - heads, L), F32)], axis=0).T
        for g in range(groups):
            hs = slice(g * per_group, (g + 1) * per_group)
            cum_s[c * groups + g] = cum_t[:, hs]
            cumt_s[c * groups + g] = cum_j[hs, :]
        seg_t = seg(base + t_iota)
        seg_q = seg(base + lax.broadcasted_iota(jnp.int32, (1, L), 1))
        allow_s[c] = jnp.where(jnp.logical_and(seg_t == seg_q, t_iota >= q_iota), 1.0, 0.0)
        since = jnp.full((L, L), 4, jnp.int32)
        for d in docs:
            gap = base + t_iota - d
            since = jnp.minimum(since, jnp.where(gap < 0, 4, gap))
        for s in range(1, K):
            keep_s[c, s - 1] = jnp.where(since < s, 0.0, 1.0)
        return 0

    lax.fori_loop(0, chunks, decays, 0, unroll=4)
    c_hi, c_mid, c_low = split3(carries[...])
    c_all = jnp.concatenate(
        [v.astype(F32) for v in (c_hi, c_mid, c_low)] + [jnp.zeros((L - 3 * heads, L), F32)], axis=0
    )
    factors[...] = dot(c_all.T.astype(BF16)[0:16, :], sel[2])

    rim = pl.ds(rows - RIM, RIM)
    spot = pl.ds(0, RIM)

    def halo(i):
        src = (x_hbm, b_hbm, c_hbm)[i].at[rim, :]
        dst = xbuf.at[spot, :] if i == 0 else bcbuf.at[i - 1, spot, :]
        return pltpu.make_async_remote_copy(
            src_ref=src,
            dst_ref=dst,
            send_sem=halo_ssem.at[i],
            recv_sem=halo_rsem.at[i],
            device_id={"ctx": lax.rem(me + 1, n_ctx)},
            device_id_type=MESH,
        )

    b_copy.wait()
    c_copy.wait()
    x_copy(0).wait()

    def conv(win, taps, keep, slot):
        w = win.astype(F32)
        cs = conv_s.at[slot]
        cs[...] = w
        half = taps * 0.5
        v = (cs[13 : 13 + L, :] * keep[2]) * half[0:1]
        v = v + (cs[14 : 14 + L, :] * keep[1]) * half[1:2]
        v = v + (cs[15 : 15 + L, :] * keep[0]) * half[2:3]
        v = v + w[16:] * half[3:4]
        return v + v * jnp.tanh(v)

    def first(g, w, c, _):
        at_start = isinstance(c, int)
        if w and not at_start:
            x_copy(c).wait()
        i = c * groups + g
        window = pl.ds(pl.multiple_of(c * L, L), L + RIM)
        keep = [keep_s[c, s] for s in range(K - 1)]
        left = left_s[c]
        mine = slice(g * N, (g + 1) * N)
        b_now = conv(bcbuf[0, window, mine], taps_b[:, mine].astype(F32), keep, 0)
        b_t = b_now.T.astype(BF16)
        c_now = conv(bcbuf[1, window, mine], taps_c[:, mine].astype(F32), keep, 1).astype(BF16)
        cconv[i] = c_now
        scores_s[i] = allow_s[c] * dot(c_now, b_t)
        wide = per_group * P_SIZE
        for at in range(0, wide, TILE):
            lanes = slice(g * wide + at, g * wide + at + TILE)
            here = slice(at, at + TILE)
            spread = dot(left, sel[0, :, lanes])
            parts = []
            for half in range(0, TILE, 128):
                sub = slice(lanes.start + half, lanes.start + half + 128)
                x_now = conv(
                    xbuf[window, sub], taps_x[:, sub].astype(F32), keep, 2 + (at + half) // 128
                )
                xconv[i, :, at + half : at + half + 128] = x_now.astype(BF16)
                parts.append((x_now * spread[:, half : half + 128]).astype(BF16))
            local = dot(b_t, jnp.concatenate(parts, axis=1))
            if at_start:
                start_s[g, :, here] = local
                continue
            factor = factors[pl.ds(c, 1), lanes]
            prefix[i + groups, :, here] = prefix[i, :, here] * factor + local
            pcar[c + 1, 0:1, lanes] = pcar[c, 0:1, lanes] * factor
        return 0

    def owner(g, q):
        if not split:
            return q * min(n_ctx, 2) + (g if n_ctx > 1 else 0)
        y, z_hi, x = lax.div(q, 4), lax.rem(lax.div(q, 2), 2), lax.rem(q, 2)
        return (y * 4 + z_hi * 2 + lax.rem(y + g, 2)) * 2 + x

    if split:
        my_y, my_z = lax.div(me, 8), lax.rem(lax.div(me, 2), 4)
        my_g = lax.rem(my_y + my_z, 2)
        my_q = (my_y * 2 + lax.div(my_z, 2)) * 2 + lax.rem(me, 2)
    else:
        my_g, my_q = lax.rem(me, 2), lax.div(me, 2)

    def owns(g):
        return my_g == g if n_ctx > 1 else True

    r_iota = lax.broadcasted_iota(jnp.int32, (16, 128), 0)

    def copy1(g, q):
        return pltpu.make_async_remote_copy(
            src_ref=send1.at[g, q],
            dst_ref=recv1.at[me],
            send_sem=ssem1.at[g],
            recv_sem=rsem1,
            device_id={"ctx": owner(g, q)},
            device_id_type=MESH,
        )

    def copy2(g, other):
        return pltpu.make_async_remote_copy(
            src_ref=send2.at[other],
            dst_ref=recv2.at[g, my_q],
            send_sem=ssem2,
            recv_sem=rsem2.at[g],
            device_id={"ctx": other},
            device_id_type=MESH,
        )

    def bulk(ref, ssem, rsem):
        return pltpu.make_async_remote_copy(
            src_ref=ref,
            dst_ref=ref,
            send_sem=ssem,
            recv_sem=rsem,
            device_id={"ctx": lax.rem(me + 1, n_ctx)},
            device_id_type=MESH,
        )

    def send_state(g):
        for pair in range(PIECES // 2):
            here = slice(pair * 128, pair * 128 + 128)
            at = g * per_group * P_SIZE + pair * 128
            hi, mid, low = split3(
                jnp.broadcast_to(
                    pcar[chunks, 0:1, at : at + 128] * factors[0:1, at : at + 128], (16, 128)
                )
            )
            tail = jnp.where(
                r_iota == 0,
                hi.astype(F32),
                jnp.where(
                    r_iota == 1, mid.astype(F32), jnp.where(r_iota == 2, low.astype(F32), 0.0)
                ),
            ).astype(BF16)
            for half in range(2):
                q, k = divmod(pair * 2 + half, per_dev)
                part = slice(half * 64, (half + 1) * 64)
                send1[g, q, k, 0:64, :] = (
                    prefix[chunks * groups + g, part, here]
                    + start_s[g, part, here] * pcar[chunks, 0:1, at : at + 128]
                ).astype(BF16)
                send1[g, q, k, 64:80, :] = tail

        def send(s, _):
            copy1(g, lax.rem(my_q + s, owners)).start()
            return 0

        if n_ctx > 1:
            lax.fori_loop(jnp.where(owns(g), 1, 0), owners, send, 0)

        @pl.when(owns(g))
        def _():
            recv1[me] = send1[g, my_q]

    def scan_state(g):
        @pl.when(owns(g))
        def _():
            if n_ctx > 1:
                bulk(recv1.at[pl.ds(0, n_ctx - 1)], ssem1.at[g], rsem1).wait_recv()

            def scan(e, acc):
                out = []
                for k in range(per_dev):
                    send2[e, k] = acc[k].astype(BF16)
                    got = recv1[e, k].astype(F32)
                    factor = got[64:65] + got[65:66] + got[66:67]
                    out.append(acc[k] * factor + got[0:64])
                return tuple(out)

            lax.fori_loop(
                0,
                n_ctx,
                scan,
                tuple(jnp.zeros((64, 128), F32) for _ in range(per_dev)),
                unroll=min(4, n_ctx),
            )

            def send_back(s, _):
                copy2(g, lax.rem(me + s, n_ctx)).start()
                return 0

            lax.fori_loop(1, n_ctx, send_back, 0)
            recv2[g, my_q] = send2[me]

    def wait_state(g):
        if n_ctx > 1:
            if owners > 1:

                @pl.when(owns(g))
                def _():
                    bulk(recv2.at[g, pl.ds(0, owners - 1)], ssem2, rsem2.at[g]).wait_recv()

            @pl.when(jnp.logical_not(owns(g)))
            def _():
                bulk(recv2.at[g], ssem2, rsem2.at[g]).wait_recv()

    def wait_sends():
        if n_ctx > 1:
            for g in range(groups):
                if owners > 1:

                    @pl.when(owns(g))
                    def _(g=g):
                        bulk(send1.at[g, pl.ds(0, owners - 1)], ssem1.at[g], rsem1).wait_send()

                @pl.when(jnp.logical_not(owns(g)))
                def _(g=g):
                    bulk(send1.at[g], ssem1.at[g], rsem1).wait_send()

            bulk(send2.at[pl.ds(0, n_ctx - 1)], ssem2, rsem2.at[0]).wait_send()

    lax.fori_loop(1, 6, functools.partial(first, 0, True), 0, unroll=2)
    pl.semaphore_wait(barrier, n_ctx + n_head - 2)
    for i in range(3):
        halo(i).start()
    lax.fori_loop(6, chunks, functools.partial(first, 0, True), 0, unroll=2)
    for i in range(3):
        halo(i).wait_recv()
    first(0, True, 0, 0)
    send_state(0)
    lax.fori_loop(1, chunks, functools.partial(first, 1, False), 0, unroll=2)
    first(1, False, 0, 0)
    send_state(1)
    scan_state(0)

    wide = per_group * P_SIZE
    for g in range(groups):
        skip_s[g, 0:1, :] = factors[chunks : chunks + 1, g * wide : (g + 1) * wide]
    lane = lax.broadcasted_iota(jnp.int32, (L, 128), 1)

    def second(i, _):
        c = lax.div(i, groups)
        scores = scores_s[i]
        cum = cum_s[i]
        for pair in range(per_group // 2):
            ws = []
            for h in (2 * pair, 2 * pair + 1):
                gap = cum[:, h : h + 1] - cumt_s[i, h : h + 1, :]
                ws.append((scores * jnp.exp2(jnp.minimum(gap, 4.0))).astype(BF16))
            x_pair = xconv[i, :, pair * 128 : (pair + 1) * 128]
            zero = jnp.zeros_like(x_pair)
            both = jnp.concatenate(
                [jnp.where(lane < P_SIZE, x_pair, zero), jnp.where(lane < P_SIZE, zero, x_pair)],
                axis=0,
            )
            here = slice(pair * 128, (pair + 1) * 128)
            yint[i, :, here] = (
                dot(jnp.concatenate(ws, axis=1), both)
                + skip_s[lax.rem(i, groups), 0:1, here] * x_pair.astype(F32)
            )
        return 0

    lax.fori_loop(0, FIRST_PART, second, 0, unroll=6)
    scan_state(1)
    lax.fori_loop(FIRST_PART, chunks * groups, second, 0, unroll=6)

    def sum_copy(part, other):
        some = pl.ds(part * 8, 8)
        return pltpu.make_async_remote_copy(
            src_ref=sums.at[some, :],
            dst_ref=sums_recv.at[my_head, some, :],
            send_sem=sum_ssem.at[part],
            recv_sem=sum_rsem.at[part],
            device_id={"head": other},
            device_id_type=MESH,
        )

    def sums_in(part):
        some = pl.ds(part * 8, 8)
        whole = sums_recv.at[pl.ds(0, n_head - 1), some, :]
        return pltpu.make_async_remote_copy(
            src_ref=whole,
            dst_ref=whole,
            send_sem=sum_ssem.at[part],
            recv_sem=sum_rsem.at[part],
            device_id={"head": lax.rem(my_head + 1, n_head)},
            device_id_type=MESH,
        )

    def send_sums(part):
        for s in range(1, n_head):
            sum_copy(part, lax.rem(my_head + s, n_head)).start()
        some = slice(part * 8, part * 8 + 8)
        sums_recv[my_head, some, :] = sums[some, :]

    def sum_row(c):
        return jnp.where(c >= chunks - 2, c + 6, c)

    def add_up(c):
        total = jnp.sum(squares_s[c].T, axis=0, keepdims=True)
        sums[pl.ds(sum_row(c), 1), :] = total

    def enter(g):
        wide = per_group * P_SIZE
        for pair in range(wide // 128):
            here = slice(pair * 128, (pair + 1) * 128)
            factor = factors[0:1, g * wide + here.start : g * wide + here.stop]
            for half in range(2):
                part = slice(half * 64, (half + 1) * 64)
                k = 2 * pair + half
                incoming = recv2[g, k // per_dev, k % per_dev].astype(F32)
                prefix[g, part, here] = incoming
                start_s[g, part, here] = start_s[g, part, here] + factor * incoming

    def third(g, c, _):
        i = c * groups + g
        r = pl.ds(pl.multiple_of(c * L, L), L)
        left = left_s[c]
        wide = per_group * P_SIZE
        squares = jnp.zeros((L, 128), F32) if g == 0 else squares_s[c]
        for at in range(0, wide, TILE):
            lanes = slice(g * wide + at, g * wide + at + TILE)
            here = slice(at, at + TILE)
            full = prefix[i, :, here] + pcar[c, 0:1, lanes] * start_s[g, :, here]
            inter = dot(cconv[i], full.astype(BF16))
            spread = dot(left, sel[1, :, lanes])
            y = yint[i, :, here] + spread * inter
            v = gate_buf[r, lanes].astype(F32) * 0.5
            gated = y * (v + v * jnp.tanh(v))
            yint[i, :, here] = gated
            sq = gated * gated
            squares = squares + sq[:, 0:128] + sq[:, 128:256]
        squares_s[c] = squares
        return 0

    def third_last(c, _):
        add_up(c - 1)
        return third(1, c, 0)

    gate_copy.wait()
    wait_state(0)
    enter(0)
    lax.fori_loop(0, chunks, functools.partial(third, 0), 0, unroll=2)
    wait_state(1)
    enter(1)
    third(1, 0, 0)
    lax.fori_loop(1, 9, third_last, 0)
    send_sums(0)
    lax.fori_loop(9, chunks - 1, third_last, 0)
    send_sums(1)
    third_last(chunks - 1, 0)
    add_up(chunks - 1)
    send_sums(2)

    wait_sends()
    for i in range(3):
        halo(i).wait_send()

    columns = n_head * heads * P_SIZE

    def norm(c, _):
        at_row = sum_row(c)
        total = sums_recv[0, pl.ds(at_row, 1), :]
        for k in range(1, n_head):
            total = total + sums_recv[k, pl.ds(at_row, 1), :]
        row = lax.rsqrt(total / columns + EPS)
        scale = jnp.broadcast_to(row, (L, L)).T
        r = pl.ds(pl.multiple_of(c * L, L), L)
        for at in range(0, x_hbm.shape[1], L):
            g, off = divmod(at, per_group * P_SIZE)
            gain = gain_ref[at : at + L].astype(F32)[None, :]
            value = yint[c * groups + g, :, off : off + L] * scale * gain
            gate_buf[r, at : at + L] = value.astype(BF16)
        return 0

    sums_in(0).wait_recv()
    lax.fori_loop(0, 8, norm, 0)
    sums_in(1).wait_recv()
    lax.fori_loop(8, chunks - 2, norm, 0)
    sums_in(2).wait_recv()
    lax.fori_loop(chunks - 2, chunks, norm, 0)
    for part in range(3):
        sums_in(part).wait_send()


def store(chunks, from_ref, out_hbm, sem):
    def copy(c):
        r = pl.ds(pl.multiple_of(c * L, L), L)
        return pltpu.make_async_copy(from_ref.at[r, :], out_hbm.at[r, :], sem.at[c])

    def begin(c, _):
        copy(c).start()
        return 0

    def finish(c, _):
        copy(c).wait()
        return 0

    lax.fori_loop(0, chunks, begin, 0)
    lax.fori_loop(0, chunks, finish, 0)


def solution(mesh):
    n_ctx = mesh.shape["ctx"]
    n_head = mesh.shape["head"]

    def shards(
        x_in, b_in, c_in, conv_x, conv_b, conv_c, step_size, decay_rate, skip, gate, norm_gain, doc_starts
    ):
        rows, cols = x_in.shape
        heads = step_size.shape[1]
        groups = b_in.shape[1] // N
        chunks = rows // L
        owners = max(n_ctx // 2, 1)
        per_dev = PIECES // owners
        wide = cols // groups
        per_group = heads // groups
        any_spec = pl.BlockSpec(memory_space=pl.ANY)
        vmem = pl.BlockSpec(memory_space=pltpu.VMEM)
        mixed = pl.pallas_call(
            functools.partial(kernel, n_ctx, n_head, chunks),
            out_shape=pltpu.VMEM((rows, cols), BF16),
            in_specs=[any_spec] * 4
            + [vmem] * 7
            + [pl.BlockSpec(memory_space=pltpu.SMEM)],
            out_specs=vmem,
            scratch_shapes=[
                pltpu.VMEM((10, L + 16, 128), F32),
                pltpu.VMEM((rows + RIM, cols), BF16),
                pltpu.VMEM((2, rows + RIM, groups * N), BF16),
                pltpu.VMEM((chunks * groups, L, wide), F32),
                pltpu.VMEM((chunks * groups, L, wide), BF16),
                pltpu.VMEM((chunks * groups, L, N), BF16),
                pltpu.VMEM(((chunks + 1) * groups, N, wide), F32),
                pltpu.VMEM((groups, N, wide), F32),
                pltpu.VMEM((chunks + 1, 8, cols), F32),
                pltpu.VMEM((chunks * heads, L), F32),
                pltpu.VMEM((chunks * groups, L, per_group), F32),
                pltpu.VMEM((chunks * groups, per_group, L), F32),
                pltpu.VMEM((chunks, L, L), F32),
                pltpu.VMEM((chunks * groups, L, L), F32),
                pltpu.VMEM((chunks, K - 1, L, L), F32),
                pltpu.VMEM((chunks, L, L), BF16),
                pltpu.VMEM((heads, L), F32),
                pltpu.VMEM((16, cols), F32),
                pltpu.VMEM((groups, 8, wide), F32),
                pltpu.VMEM((3, L, cols), BF16),
                pltpu.VMEM((groups, owners, per_dev, ROWS, 128), BF16),
                pltpu.VMEM((n_ctx, per_dev, ROWS, 128), BF16),
                pltpu.VMEM((n_ctx, per_dev, 64, 128), BF16),
                pltpu.VMEM((groups, owners, per_dev, 64, 128), BF16),
                pltpu.VMEM((chunks, L, 128), F32),
                pltpu.VMEM((24, L), F32),
                pltpu.VMEM((n_head, 24, L), F32),
                pltpu.SemaphoreType.DMA((chunks,)),
                pltpu.SemaphoreType.DMA((2,)),
                pltpu.SemaphoreType.DMA,
                pltpu.SemaphoreType.DMA((3,)),
                pltpu.SemaphoreType.DMA((3,)),
                pltpu.SemaphoreType.DMA((groups,)),
                pltpu.SemaphoreType.DMA,
                pltpu.SemaphoreType.DMA,
                pltpu.SemaphoreType.DMA((groups,)),
                pltpu.SemaphoreType.DMA((3,)),
                pltpu.SemaphoreType.DMA((3,)),
            ],
            compiler_params=pltpu.CompilerParams(
                collective_id=0, has_side_effects=True, vmem_limit_bytes=57 * 1024 * 1024 + 512 * 1024
            ),
        )(
            x_in,
            b_in,
            c_in,
            gate,
            conv_x,
            conv_b,
            conv_c,
            step_size.T,
            decay_rate.reshape(1, -1),
            skip.reshape(1, -1),
            norm_gain,
            doc_starts,
        )
        return pl.pallas_call(
            functools.partial(store, chunks),
            out_shape=jax.ShapeDtypeStruct((rows, cols), BF16),
            in_specs=[vmem],
            out_specs=any_spec,
            scratch_shapes=[pltpu.SemaphoreType.DMA((chunks,))],
            compiler_params=pltpu.CompilerParams(vmem_limit_bytes=24 * 1024 * 1024),
        )(mixed)

    split = P("ctx", "head")
    taps = P(None, "head")
    line = P("head")
    return jax.shard_map(
        shards,
        mesh=mesh,
        in_specs=(split,) * 3 + (taps,) * 3 + (split, line, line, split, line, P()),
        out_specs=split,
        check_vma=False,
    )
```

```python
import functools
import math

import jax
import jax.numpy as jnp
from jax import lax
from jax.experimental import pallas as pl
from jax.experimental.pallas import tpu as pltpu
from jax.sharding import PartitionSpec as P

F32 = jnp.float32
BF16 = jnp.bfloat16
P_SIZE = 64
N = 128
K = 4
RIM = 16
L = 128
TILE = 256
EPS = 1e-05
LOG2E = math.log2(math.e)
HI = lax.Precision.HIGHEST
MESH = pl.DeviceIdType.MESH
PIECES = 16
ROWS = 80
FIRST_PART = 24


def split3(v):
    hi = v.astype(BF16)
    rest = v - hi.astype(F32)
    mid = rest.astype(BF16)
    low = (rest - mid.astype(F32)).astype(BF16)
    return hi, mid, low


def dot(a, b, **kw):
    return jnp.dot(a, b, preferred_element_type=F32, **kw)


def kernel(
    n_ctx,
    n_head,
    chunks,
    x_hbm,
    b_hbm,
    c_hbm,
    gate_hbm,
    taps_x,
    taps_b,
    taps_c,
    step_ref,
    rate_ref,
    skip_ref,
    gain_ref,
    doc_ref,
    gate_buf,
    conv_s,
    xbuf,
    bcbuf,
    yint,
    xconv,
    cconv,
    prefix,
    start_s,
    pcar,
    cum_all,
    cum_s,
    cumt_s,
    allow_s,
    scores_s,
    left_s,
    carries,
    factors,
    skip_s,
    sel,
    send1,
    recv1,
    send2,
    recv2,
    sums,
    sums_recv,
    x_sem,
    bc_sem,
    gate_sem,
    halo_ssem,
    halo_rsem,
    ssem1,
    rsem1,
    ssem2,
    rsem2,
    sum_ssem,
    sum_rsem,
):
    me = lax.axis_index("ctx")
    my_head = lax.axis_index("head")
    rows = chunks * L
    heads = step_ref.shape[0]
    owners = max(n_ctx // 2, 1)
    per_dev = PIECES // owners
    split = n_ctx == 32

    def x_copy(c):
        r = pl.ds(pl.multiple_of(c * L, L), L)
        d = pl.ds(pl.multiple_of(c * L + RIM, RIM), L)
        return pltpu.make_async_copy(x_hbm.at[r, :], xbuf.at[d, :], x_sem.at[c])

    gate_copy = pltpu.make_async_copy(gate_hbm, gate_buf, gate_sem)
    b_copy = pltpu.make_async_copy(b_hbm, bcbuf.at[0, pl.ds(RIM, rows), :], bc_sem.at[0])
    c_copy = pltpu.make_async_copy(c_hbm, bcbuf.at[1, pl.ds(RIM, rows), :], bc_sem.at[1])
    b_copy.start()
    c_copy.start()

    def start_x(c, _):
        x_copy(c).start()
        return 0

    lax.fori_loop(0, chunks, start_x, 0)
    gate_copy.start()

    barrier = pltpu.get_barrier_semaphore()

    def greet_ctx(s, _):
        pl.semaphore_signal(
            barrier, inc=1, device_id={"ctx": lax.rem(me + s, n_ctx)}, device_id_type=MESH
        )
        return 0

    def greet_head(s, _):
        pl.semaphore_signal(
            barrier, inc=1, device_id={"head": lax.rem(my_head + s, n_head)}, device_id_type=MESH
        )
        return 0

    lax.fori_loop(1, n_ctx, greet_ctx, 0)
    lax.fori_loop(1, n_head, greet_head, 0)

    sel_row = lax.broadcasted_iota(jnp.int32, (L, x_hbm.shape[1]), 0)
    sel_lane = lax.broadcasted_iota(jnp.int32, (L, x_hbm.shape[1]), 1)
    chosen = jnp.where((sel_row & (heads - 1)) == (sel_lane >> 6), 1.0, 0.0)
    sel[0] = jnp.where(sel_row < 2 * heads, chosen, 0.0).astype(BF16)
    sel[1] = jnp.where(sel_row >= 2 * heads, chosen, 0.0).astype(BF16)
    sel[2] = jnp.where(sel_row < 3 * heads, chosen, 0.0).astype(BF16)
    t_iota = lax.broadcasted_iota(jnp.int32, (L, L), 0)
    q_iota = lax.broadcasted_iota(jnp.int32, (L, L), 1)
    pcar[0, 0:1, :] = jnp.zeros((1, pcar.shape[2]), F32)
    pcar[1, 0:1, :] = jnp.ones((1, pcar.shape[2]), F32)
    sums[...] = jnp.zeros_like(sums)
    groups = cconv.shape[0] // chunks
    per_group = heads // groups
    prefix[groups : 2 * groups] = jnp.zeros((groups,) + prefix.shape[1:], F32)
    docs = [doc_ref[d] for d in range(doc_ref.shape[0])]

    def seg(pos):
        total = jnp.where(pos >= docs[0], 1, 0)
        for d in docs[1:]:
            total = total + jnp.where(pos >= d, 1, 0)
        return total

    eye = lax.broadcasted_iota(jnp.int32, (heads, heads), 0) == lax.broadcasted_iota(
        jnp.int32, (heads, heads), 1
    )

    def column(row):
        return jnp.sum(
            jnp.where(eye, jnp.broadcast_to(row, (heads, heads)), 0.0), axis=1, keepdims=True
        )

    rate = column(rate_ref[...]) * -LOG2E
    steps = [step_ref[:, c * L : (c + 1) * L] for c in range(chunks)]
    triu = jnp.where(t_iota <= q_iota, 1.0, 0.0)
    cum_all[...] = dot(jnp.concatenate([v * rate for v in steps], axis=0), triu, precision=HI)
    carries[...] = jnp.where(
        lax.broadcasted_iota(jnp.int32, (heads, L), 1) == chunks, column(skip_ref[...]), 0.0
    )

    def decays(c, _):
        base = me * rows + c * L
        here = pl.ds(pl.multiple_of(c * heads, heads), heads)
        cum = cum_all[here, :]
        step = step_ref[:, pl.ds(pl.multiple_of(c * L, L), L)]
        cum_j = cum - jnp.log(step) * LOG2E
        h_lane = lax.broadcasted_iota(jnp.int32, (heads, L), 1)
        seg_j = seg(base + h_lane)
        seg_last = seg(base + L - 1)
        seg_before = seg(base - 1)
        last = cum[:, L - 1 : L]
        weight = jnp.where(seg_j == seg_last, jnp.exp2(last - cum_j), 0.0)
        inflow = jnp.where(seg_j == seg_before, jnp.exp2(cum), 0.0)
        carry = jnp.where(seg_last == seg_before, jnp.exp2(last), 0.0)
        carries[...] = jnp.where(h_lane == c, carry, carries[...])
        w_hi = weight.astype(BF16).astype(F32)
        i_hi = inflow.astype(BF16).astype(F32)
        stack = jnp.concatenate([w_hi, weight - w_hi, i_hi, inflow - i_hi], axis=0)
        left_s[c] = stack.T.astype(BF16)
        cum_t = jnp.concatenate([cum, jnp.zeros((L - heads, L), F32)], axis=0).T
        for g in range(groups):
            hs = slice(g * per_group, (g + 1) * per_group)
            cum_s[c * groups + g] = cum_t[:, hs]
            cumt_s[c * groups + g] = cum_j[hs, :]
        seg_t = seg(base + t_iota)
        seg_q = seg(base + lax.broadcasted_iota(jnp.int32, (1, L), 1))
        allow_s[c] = jnp.where(jnp.logical_and(seg_t == seg_q, t_iota >= q_iota), 1.0, 0.0)
        since = jnp.full((L, L), 4, jnp.int32)
        for d in docs:
            gap = base + t_iota - d
            since = jnp.minimum(since, jnp.where(gap < 0, 4, gap))
        for s in range(1, K):
            yint[c, :, (s - 1) * L : s * L] = jnp.where(since < s, 0.0, 1.0)
        return 0

    lax.fori_loop(0, chunks, decays, 0, unroll=4)
    c_hi, c_mid, c_low = split3(carries[...])
    c_all = jnp.concatenate(
        [v.astype(F32) for v in (c_hi, c_mid, c_low)] + [jnp.zeros((L - 3 * heads, L), F32)], axis=0
    )
    factors[...] = dot(c_all.T.astype(BF16)[0:16, :], sel[2])

    rim = pl.ds(rows - RIM, RIM)
    spot = pl.ds(0, RIM)

    def halo(i):
        src = (x_hbm, b_hbm, c_hbm)[i].at[rim, :]
        dst = xbuf.at[spot, :] if i == 0 else bcbuf.at[i - 1, spot, :]
        return pltpu.make_async_remote_copy(
            src_ref=src,
            dst_ref=dst,
            send_sem=halo_ssem.at[i],
            recv_sem=halo_rsem.at[i],
            device_id={"ctx": lax.rem(me + 1, n_ctx)},
            device_id_type=MESH,
        )

    b_copy.wait()
    c_copy.wait()
    x_copy(0).wait()

    def conv(win, taps, keep, slot):
        w = win.astype(F32)
        cs = conv_s.at[slot]
        cs[...] = w
        half = taps * 0.5
        v = (cs[13 : 13 + L, :] * keep[2]) * half[0:1]
        v = v + (cs[14 : 14 + L, :] * keep[1]) * half[1:2]
        v = v + (cs[15 : 15 + L, :] * keep[0]) * half[2:3]
        v = v + w[16:] * half[3:4]
        return v + v * jnp.tanh(v)

    def first(g, w, c, _):
        at_start = isinstance(c, int)
        if w and not at_start:
            x_copy(c).wait()
        i = c * groups + g
        window = pl.ds(pl.multiple_of(c * L, L), L + RIM)
        keep = [yint[c, :, s * L : (s + 1) * L] for s in range(K - 1)]
        left = left_s[c]
        mine = slice(g * N, (g + 1) * N)
        b_now = conv(bcbuf[0, window, mine], taps_b[:, mine].astype(F32), keep, 0)
        b_t = b_now.T.astype(BF16)
        c_now = conv(bcbuf[1, window, mine], taps_c[:, mine].astype(F32), keep, 1).astype(BF16)
        cconv[i] = c_now
        scores_s[i] = allow_s[c] * dot(c_now, b_t)
        wide = per_group * P_SIZE
        for at in range(0, wide, TILE):
            lanes = slice(g * wide + at, g * wide + at + TILE)
            here = slice(at, at + TILE)
            spread = dot(left, sel[0, :, lanes])
            parts = []
            for half in range(0, TILE, 128):
                sub = slice(lanes.start + half, lanes.start + half + 128)
                x_now = conv(
                    xbuf[window, sub], taps_x[:, sub].astype(F32), keep, 2 + (at + half) // 128
                )
                xconv[i, :, at + half : at + half + 128] = x_now.astype(BF16)
                parts.append((x_now * spread[:, half : half + 128]).astype(BF16))
            local = dot(b_t, jnp.concatenate(parts, axis=1))
            if at_start:
                start_s[g, :, here] = local
                continue
            factor = factors[pl.ds(c, 1), lanes]
            prefix[i + groups, :, here] = prefix[i, :, here] * factor + local
            pcar[c + 1, 0:1, lanes] = pcar[c, 0:1, lanes] * factor
        return 0

    def owner(g, q):
        if not split:
            return q * min(n_ctx, 2) + (g if n_ctx > 1 else 0)
        y, z_hi, x = lax.div(q, 4), lax.rem(lax.div(q, 2), 2), lax.rem(q, 2)
        return (y * 4 + z_hi * 2 + lax.rem(y + g, 2)) * 2 + x

    if split:
        my_y, my_z = lax.div(me, 8), lax.rem(lax.div(me, 2), 4)
        my_g = lax.rem(my_y + my_z, 2)
        my_q = (my_y * 2 + lax.div(my_z, 2)) * 2 + lax.rem(me, 2)
    else:
        my_g, my_q = lax.rem(me, 2), lax.div(me, 2)

    def owns(g):
        return my_g == g if n_ctx > 1 else True

    r_iota = lax.broadcasted_iota(jnp.int32, (16, 128), 0)

    def copy1(g, q):
        return pltpu.make_async_remote_copy(
            src_ref=send1.at[g, q],
            dst_ref=recv1.at[me],
            send_sem=ssem1.at[g],
            recv_sem=rsem1,
            device_id={"ctx": owner(g, q)},
            device_id_type=MESH,
        )

    def copy2(g, other):
        return pltpu.make_async_remote_copy(
            src_ref=send2.at[other],
            dst_ref=recv2.at[g, my_q],
            send_sem=ssem2,
            recv_sem=rsem2.at[g],
            device_id={"ctx": other},
            device_id_type=MESH,
        )

    def bulk(ref, ssem, rsem):
        return pltpu.make_async_remote_copy(
            src_ref=ref,
            dst_ref=ref,
            send_sem=ssem,
            recv_sem=rsem,
            device_id={"ctx": lax.rem(me + 1, n_ctx)},
            device_id_type=MESH,
        )

    def send_state(g):
        for pair in range(PIECES // 2):
            here = slice(pair * 128, pair * 128 + 128)
            at = g * per_group * P_SIZE + pair * 128
            hi, mid, low = split3(
                jnp.broadcast_to(
                    pcar[chunks, 0:1, at : at + 128] * factors[0:1, at : at + 128], (16, 128)
                )
            )
            tail = jnp.where(
                r_iota == 0,
                hi.astype(F32),
                jnp.where(
                    r_iota == 1, mid.astype(F32), jnp.where(r_iota == 2, low.astype(F32), 0.0)
                ),
            ).astype(BF16)
            for half in range(2):
                q, k = divmod(pair * 2 + half, per_dev)
                part = slice(half * 64, (half + 1) * 64)
                send1[g, q, k, 0:64, :] = (
                    prefix[chunks * groups + g, part, here]
                    + start_s[g, part, here] * pcar[chunks, 0:1, at : at + 128]
                ).astype(BF16)
                send1[g, q, k, 64:80, :] = tail

        def send(s, _):
            copy1(g, lax.rem(my_q + s, owners)).start()
            return 0

        if n_ctx > 1:
            lax.fori_loop(jnp.where(owns(g), 1, 0), owners, send, 0)

        @pl.when(owns(g))
        def _():
            recv1[me] = send1[g, my_q]

    def scan_state(g):
        @pl.when(owns(g))
        def _():
            if n_ctx > 1:
                bulk(recv1.at[pl.ds(0, n_ctx - 1)], ssem1.at[g], rsem1).wait_recv()

            def scan(e, acc):
                out = []
                for k in range(per_dev):
                    send2[e, k] = acc[k].astype(BF16)
                    got = recv1[e, k].astype(F32)
                    factor = got[64:65] + got[65:66] + got[66:67]
                    out.append(acc[k] * factor + got[0:64])
                return tuple(out)

            lax.fori_loop(
                0,
                n_ctx,
                scan,
                tuple(jnp.zeros((64, 128), F32) for _ in range(per_dev)),
                unroll=min(4, n_ctx),
            )

            def send_back(s, _):
                copy2(g, lax.rem(me + s, n_ctx)).start()
                return 0

            lax.fori_loop(1, n_ctx, send_back, 0)
            recv2[g, my_q] = send2[me]

    def wait_state(g):
        if n_ctx > 1:
            if owners > 1:

                @pl.when(owns(g))
                def _():
                    bulk(recv2.at[g, pl.ds(0, owners - 1)], ssem2, rsem2.at[g]).wait_recv()

            @pl.when(jnp.logical_not(owns(g)))
            def _():
                bulk(recv2.at[g], ssem2, rsem2.at[g]).wait_recv()

    def wait_sends():
        if n_ctx > 1:
            for g in range(groups):
                if owners > 1:

                    @pl.when(owns(g))
                    def _(g=g):
                        bulk(send1.at[g, pl.ds(0, owners - 1)], ssem1.at[g], rsem1).wait_send()

                @pl.when(jnp.logical_not(owns(g)))
                def _(g=g):
                    bulk(send1.at[g], ssem1.at[g], rsem1).wait_send()

            bulk(send2.at[pl.ds(0, n_ctx - 1)], ssem2, rsem2.at[0]).wait_send()

    lax.fori_loop(1, 6, functools.partial(first, 0, True), 0, unroll=2)
    pl.semaphore_wait(barrier, n_ctx + n_head - 2)
    for i in range(3):
        halo(i).start()
    lax.fori_loop(6, chunks, functools.partial(first, 0, True), 0, unroll=2)
    for i in range(3):
        halo(i).wait_recv()
    first(0, True, 0, 0)
    send_state(0)
    lax.fori_loop(1, chunks, functools.partial(first, 1, False), 0, unroll=2)
    first(1, False, 0, 0)
    send_state(1)
    scan_state(0)

    wide = per_group * P_SIZE
    for g in range(groups):
        skip_s[g, 0:1, :] = factors[chunks : chunks + 1, g * wide : (g + 1) * wide]
    lane = lax.broadcasted_iota(jnp.int32, (L, 128), 1)

    def second(i, _):
        c = lax.div(i, groups)
        scores = scores_s[i]
        cum = cum_s[i]
        for pair in range(per_group // 2):
            ws = []
            for h in (2 * pair, 2 * pair + 1):
                gap = cum[:, h : h + 1] - cumt_s[i, h : h + 1, :]
                ws.append((scores * jnp.exp2(jnp.minimum(gap, 4.0))).astype(BF16))
            x_pair = xconv[i, :, pair * 128 : (pair + 1) * 128]
            zero = jnp.zeros_like(x_pair)
            both = jnp.concatenate(
                [jnp.where(lane < P_SIZE, x_pair, zero), jnp.where(lane < P_SIZE, zero, x_pair)],
                axis=0,
            )
            here = slice(pair * 128, (pair + 1) * 128)
            yint[i, :, here] = (
                dot(jnp.concatenate(ws, axis=1), both)
                + skip_s[lax.rem(i, groups), 0:1, here] * x_pair.astype(F32)
            )
        return 0

    lax.fori_loop(0, FIRST_PART, second, 0, unroll=6)
    scan_state(1)
    lax.fori_loop(FIRST_PART, chunks * groups, second, 0, unroll=6)

    def sum_copy(part, other):
        some = pl.ds(part * 8, 8)
        return pltpu.make_async_remote_copy(
            src_ref=sums.at[some, :],
            dst_ref=sums_recv.at[my_head, some, :],
            send_sem=sum_ssem.at[part],
            recv_sem=sum_rsem.at[part],
            device_id={"head": other},
            device_id_type=MESH,
        )

    def sums_in(part):
        some = pl.ds(part * 8, 8)
        whole = sums_recv.at[pl.ds(0, n_head - 1), some, :]
        return pltpu.make_async_remote_copy(
            src_ref=whole,
            dst_ref=whole,
            send_sem=sum_ssem.at[part],
            recv_sem=sum_rsem.at[part],
            device_id={"head": lax.rem(my_head + 1, n_head)},
            device_id_type=MESH,
        )

    def send_sums(part):
        for s in range(1, n_head):
            sum_copy(part, lax.rem(my_head + s, n_head)).start()
        some = slice(part * 8, part * 8 + 8)
        sums_recv[my_head, some, :] = sums[some, :]

    def sum_row(c):
        return jnp.where(c >= chunks - 2, c + 6, c)

    def add_up(c):
        total = jnp.sum(allow_s[c].T, axis=0, keepdims=True)
        sums[pl.ds(sum_row(c), 1), :] = total

    def enter(g):
        wide = per_group * P_SIZE
        for pair in range(wide // 128):
            here = slice(pair * 128, (pair + 1) * 128)
            factor = factors[0:1, g * wide + here.start : g * wide + here.stop]
            for half in range(2):
                part = slice(half * 64, (half + 1) * 64)
                k = 2 * pair + half
                incoming = recv2[g, k // per_dev, k % per_dev].astype(F32)
                prefix[g, part, here] = incoming
                start_s[g, part, here] = start_s[g, part, here] + factor * incoming

    def third(g, c, _):
        i = c * groups + g
        r = pl.ds(pl.multiple_of(c * L, L), L)
        left = left_s[c]
        wide = per_group * P_SIZE
        squares = jnp.zeros((L, 128), F32) if g == 0 else allow_s[c]
        for at in range(0, wide, TILE):
            lanes = slice(g * wide + at, g * wide + at + TILE)
            here = slice(at, at + TILE)
            full = prefix[i, :, here] + pcar[c, 0:1, lanes] * start_s[g, :, here]
            inter = dot(cconv[i], full.astype(BF16))
            spread = dot(left, sel[1, :, lanes])
            y = yint[i, :, here] + spread * inter
            v = gate_buf[r, lanes].astype(F32) * 0.5
            gated = y * (v + v * jnp.tanh(v))
            yint[i, :, here] = gated
            sq = gated * gated
            squares = squares + sq[:, 0:128] + sq[:, 128:256]
        allow_s[c] = squares
        return 0

    def third_last(c, _):
        add_up(c - 1)
        return third(1, c, 0)

    gate_copy.wait()
    wait_state(0)
    enter(0)
    lax.fori_loop(0, chunks, functools.partial(third, 0), 0, unroll=2)
    wait_state(1)
    enter(1)
    third(1, 0, 0)
    lax.fori_loop(1, 9, third_last, 0, unroll=2)
    send_sums(0)
    lax.fori_loop(9, chunks - 1, third_last, 0, unroll=2)
    send_sums(1)
    third_last(chunks - 1, 0)
    add_up(chunks - 1)
    send_sums(2)

    wait_sends()
    for i in range(3):
        halo(i).wait_send()

    columns = n_head * heads * P_SIZE

    def norm(c, _):
        at_row = sum_row(c)
        total = sums_recv[0, pl.ds(at_row, 1), :]
        for k in range(1, n_head):
            total = total + sums_recv[k, pl.ds(at_row, 1), :]
        row = lax.rsqrt(total / columns + EPS)
        scale = jnp.broadcast_to(row, (L, L)).T
        r = pl.ds(pl.multiple_of(c * L, L), L)
        for at in range(0, x_hbm.shape[1], L):
            g, off = divmod(at, per_group * P_SIZE)
            gain = gain_ref[at : at + L].astype(F32)[None, :]
            value = yint[c * groups + g, :, off : off + L] * scale * gain
            gate_buf[r, at : at + L] = value.astype(BF16)
        return 0

    sums_in(0).wait_recv()
    lax.fori_loop(0, 8, norm, 0, unroll=2)
    sums_in(1).wait_recv()
    lax.fori_loop(8, chunks - 2, norm, 0, unroll=2)
    sums_in(2).wait_recv()
    lax.fori_loop(chunks - 2, chunks, norm, 0, unroll=2)
    for part in range(3):
        sums_in(part).wait_send()


def store(chunks, from_ref, out_hbm, sem):
    def copy(c):
        r = pl.ds(pl.multiple_of(c * L, L), L)
        return pltpu.make_async_copy(from_ref.at[r, :], out_hbm.at[r, :], sem.at[c])

    def begin(c, _):
        copy(c).start()
        return 0

    def finish(c, _):
        copy(c).wait()
        return 0

    lax.fori_loop(0, chunks, begin, 0)
    lax.fori_loop(0, chunks, finish, 0)


def solution(mesh):
    n_ctx = mesh.shape["ctx"]
    n_head = mesh.shape["head"]

    def shards(
        x_in, b_in, c_in, conv_x, conv_b, conv_c, step_size, decay_rate, skip, gate, norm_gain, doc_starts
    ):
        rows, cols = x_in.shape
        heads = step_size.shape[1]
        groups = b_in.shape[1] // N
        chunks = rows // L
        owners = max(n_ctx // 2, 1)
        per_dev = PIECES // owners
        wide = cols // groups
        per_group = heads // groups
        any_spec = pl.BlockSpec(memory_space=pl.ANY)
        vmem = pl.BlockSpec(memory_space=pltpu.VMEM)
        mixed = pl.pallas_call(
            functools.partial(kernel, n_ctx, n_head, chunks),
            out_shape=pltpu.VMEM((rows, cols), BF16),
            in_specs=[any_spec] * 4
            + [vmem] * 7
            + [pl.BlockSpec(memory_space=pltpu.SMEM)],
            out_specs=vmem,
            scratch_shapes=[
                pltpu.VMEM((10, L + 16, 128), F32),
                pltpu.VMEM((rows + RIM, cols), BF16),
                pltpu.VMEM((2, rows + RIM, groups * N), BF16),
                pltpu.VMEM((chunks * groups, L, wide), F32),
                pltpu.VMEM((chunks * groups, L, wide), BF16),
                pltpu.VMEM((chunks * groups, L, N), BF16),
                pltpu.VMEM(((chunks + 1) * groups, N, wide), F32),
                pltpu.VMEM((groups, N, wide), F32),
                pltpu.VMEM((chunks + 1, 8, cols), F32),
                pltpu.VMEM((chunks * heads, L), F32),
                pltpu.VMEM((chunks * groups, L, per_group), F32),
                pltpu.VMEM((chunks * groups, per_group, L), F32),
                pltpu.VMEM((chunks, L, L), F32),
                pltpu.VMEM((chunks * groups, L, L), F32),
                pltpu.VMEM((chunks, L, L), BF16),
                pltpu.VMEM((heads, L), F32),
                pltpu.VMEM((16, cols), F32),
                pltpu.VMEM((groups, 8, wide), F32),
                pltpu.VMEM((3, L, cols), BF16),
                pltpu.VMEM((groups, owners, per_dev, ROWS, 128), BF16),
                pltpu.VMEM((n_ctx, per_dev, ROWS, 128), BF16),
                pltpu.VMEM((n_ctx, per_dev, 64, 128), BF16),
                pltpu.VMEM((groups, owners, per_dev, 64, 128), BF16),
                pltpu.VMEM((24, L), F32),
                pltpu.VMEM((n_head, 24, L), F32),
                pltpu.SemaphoreType.DMA((chunks,)),
                pltpu.SemaphoreType.DMA((2,)),
                pltpu.SemaphoreType.DMA,
                pltpu.SemaphoreType.DMA((3,)),
                pltpu.SemaphoreType.DMA((3,)),
                pltpu.SemaphoreType.DMA((groups,)),
                pltpu.SemaphoreType.DMA,
                pltpu.SemaphoreType.DMA,
                pltpu.SemaphoreType.DMA((groups,)),
                pltpu.SemaphoreType.DMA((3,)),
                pltpu.SemaphoreType.DMA((3,)),
            ],
            compiler_params=pltpu.CompilerParams(
                collective_id=0, has_side_effects=True, vmem_limit_bytes=57 * 1024 * 1024 + 512 * 1024
            ),
        )(
            x_in,
            b_in,
            c_in,
            gate,
            conv_x,
            conv_b,
            conv_c,
            step_size.T,
            decay_rate.reshape(1, -1),
            skip.reshape(1, -1),
            norm_gain,
            doc_starts,
        )
        return pl.pallas_call(
            functools.partial(store, chunks),
            out_shape=jax.ShapeDtypeStruct((rows, cols), BF16),
            in_specs=[vmem],
            out_specs=any_spec,
            scratch_shapes=[pltpu.SemaphoreType.DMA((chunks,))],
            compiler_params=pltpu.CompilerParams(vmem_limit_bytes=24 * 1024 * 1024),
        )(mixed)

    split = P("ctx", "head")
    taps = P(None, "head")
    line = P("head")
    return jax.shard_map(
        shards,
        mesh=mesh,
        in_specs=(split,) * 3 + (taps,) * 3 + (split, line, line, split, line, P()),
        out_specs=split,
        check_vma=False,
    )
```
